32 devices in a mesh: ctx: 16 (over z, y, x), tp: 2 (over core).
Axes of the slice: x: 2, y: 2, z: 4, core: 2. Of those that a mesh axis runs over, the one named last changes fastest.
Arguments:
- queries: bfloat16 [4096, 8192], P('ctx', 'tp'), may hold values from -6 to 6
- key_branch: bfloat16 [4096, 8192], P('ctx', 'tp'), may hold values from -6 to 6
- value_branch: bfloat16 [4096, 8192], P('ctx', 'tp'), may hold values from -6 to 6
- cotangent: bfloat16 [4096, 8192], P('ctx', 'tp'), may hold values from -6 to 6
- filters: float32 [512, 128], replicated, may hold values from -0.5 to 0.5
- skip_bias: float32 [8192], P('tp'), may hold values from -1 to 1
- contig_start: int32 [4096], replicated, may hold values from 0 to 4095, as said below
Outputs:
- output: bfloat16 [4096, 8192], P('ctx', 'tp')
- grad_query: bfloat16 [4096, 8192], P('ctx', 'tp')
- grad_key: bfloat16 [4096, 8192], P('ctx', 'tp')
- grad_value: bfloat16 [4096, 8192], P('ctx', 'tp')
- grad_filter: float32 [512, 128], replicated
- grad_bias: float32 [8192], P('tp')
The draws below stay inside these ranges and needn't reach their ends.
Inputs may be any that keep to these rules, and one draw needn't show every extreme that they name: contig_start[0] is 0, and for t > 0 contig_start[t] is either t (a new contig begins) or contig_start[t - 1]; the last token begins a contig of its own.
All inputs are finite; a program needn't handle non-finite values.
Results may differ from the reference program's by a relative error of at most 0.0056.
Values may be sent and summed in bfloat16 or wider, within the bound.
No kernel may reach another device: no remote copies, remote signals or barrier semaphores. Data moves between devices by JAX's collectives and lax.ppermute only.
A program may use at most 128 MiB of HBM per device.

```python
import math
import jax
import jax.numpy as jnp
from jax import lax

D = 8192
FILT = 128
GROUPS = 512
TOKENS = 4096


def draw_contig_start(key, part):
    positions = jnp.arange(TOKENS, dtype=jnp.int32)
    marks = jax.random.randint(jax.random.fold_in(key, 17), (TOKENS,), 0, 256) == 0
    marks = jnp.where(positions == 0, True, marks)
    marks = jnp.where(positions == TOKENS - 1, True, marks)
    return lax.cummax(jnp.where(marks, positions, 0), axis=0)


def block_levels(key, extent, cuts, low, high):
    gain, own = 1.0, jax.random.fold_in(key, 6)
    for position, blocks in cuts:
        draws = jnp.exp(jax.random.uniform(jax.random.fold_in(own, position), (blocks,), jnp.float32, low / len(cuts), high / len(cuts)))
        gain = gain * jnp.repeat(draws, extent[position] // blocks).reshape([-1 if axis == position else 1 for axis in range(len(extent))])
    return gain


def noise(key, dims, scale, reach, shards=(), kind=jnp.bfloat16):
    values = scale * jax.random.normal(key, dims, jnp.float32)
    if shards:
        values = values * block_levels(key, dims, shards, -0.22, 0.18)
    return jnp.clip(values, -reach, reach).astype(kind)


def setup_inputs(seed: int = 0) -> dict:
    key_of = jax.random.split(jax.random.key(seed), 8)
    queries = noise(key_of[0], (TOKENS, D), 1.0, 6.0, ((0, 16), (1, 2)))
    key_branch = noise(key_of[1], (TOKENS, D), 1.0, 6.0, ((0, 16), (1, 2)))
    value_branch = noise(key_of[2], (TOKENS, D), 1.0, 6.0, ((0, 16), (1, 2)))
    cotangent = noise(key_of[3], (TOKENS, D), 1.0, 6.0, ((0, 16), (1, 2)))
    filters = noise(key_of[4], (GROUPS, FILT), FILT ** -0.5, 0.5, (), jnp.float32)
    skip_bias = jnp.clip(jax.random.uniform(key_of[5], (D,), jnp.float32, -1.0, 1.0) * block_levels(key_of[5], (D,), ((0, 2),), -0.4, 0.0), -1.0, 1.0)
    contig_start = draw_contig_start(jax.random.fold_in(key_of[7], 71), 0)
    return {"queries": queries, "key_branch": key_branch, "value_branch": value_branch, "cotangent": cotangent, "filters": filters, "skip_bias": skip_bias, "contig_start": contig_start}


def toeplitz(filter_taps):
    group_count, filter_size = filter_taps.shape
    leading = jnp.zeros((group_count, 1), filter_taps.dtype)
    trailing = jnp.zeros((group_count, filter_size), filter_taps.dtype)
    pattern = jnp.concatenate([leading, filter_taps[:, ::-1], trailing], axis=1)
    tiled = jnp.tile(pattern, (1, filter_size))[:, :2 * filter_size * filter_size]
    return tiled.reshape(group_count, filter_size, 2 * filter_size)

def fold_lags(products):
    filter_size, window_size = products.shape
    flattened = products.reshape(filter_size * window_size)
    flattened = jnp.concatenate([flattened, jnp.zeros((filter_size,), products.dtype)])
    columns = flattened.reshape(filter_size, window_size + 1).sum(axis=0)
    return columns[1:filter_size + 1][::-1]

def reference(queries, key_branch, value_branch, cotangent, filters, skip_bias, contig_start):
    token_count, channel_count = queries.shape
    group_count, filter_size = filters.shape
    per_group = channel_count // group_count
    block_count = token_count // filter_size
    gated_signal = (key_branch.astype(jnp.float32) * value_branch.astype(jnp.float32)).astype(jnp.bfloat16)
    signal_grad = (cotangent.astype(jnp.float32) * queries.astype(jnp.float32)).astype(jnp.bfloat16)
    filter_taps = lax.optimization_barrier(filters.astype(jnp.bfloat16)).astype(jnp.float32)
    band_all = toeplitz(filter_taps)
    row_starts = jnp.concatenate([contig_start.astype(jnp.int32), jnp.zeros((filter_size,), jnp.int32)])
    row_starts = row_starts.reshape(block_count + 1, filter_size)
    source_pos = (jnp.arange(block_count + 1, dtype=jnp.int32)[:, None] - 1) * filter_size
    source_pos = source_pos + jnp.arange(2 * filter_size, dtype=jnp.int32)[None, :]
    visible = source_pos[:, None, :] >= row_starts[:, :, None]

    def one_group(group):
        first_col = (group * per_group).astype(jnp.int32)

        def columns(array):
            return lax.dynamic_slice_in_dim(array, first_col, per_group, 1).astype(jnp.float32)
        query_part = columns(queries)
        key_part = columns(key_branch)
        value_part = columns(value_branch)
        cotangent_part = columns(cotangent)
        signal_part = columns(gated_signal)
        grad_part = columns(signal_grad)
        bias_part = lax.dynamic_slice_in_dim(skip_bias, first_col, per_group, 0).astype(jnp.float32)
        padded = jnp.concatenate([jnp.zeros((filter_size, per_group), jnp.float32), signal_part], axis=0)
        windows = jnp.concatenate([padded[:token_count].reshape(block_count, filter_size, per_group), padded[filter_size:].reshape(block_count, filter_size, per_group)], axis=1)
        grads_ext = jnp.concatenate([grad_part, jnp.zeros((filter_size, per_group), jnp.float32)], axis=0)
        grads_ext = grads_ext.reshape(block_count + 1, filter_size, per_group)
        band = jnp.where(visible, band_all[group][None], jnp.zeros((), jnp.float32))
        convolved = jnp.einsum('bts,bsc->btc', band[:block_count], windows).reshape(token_count, per_group)
        back_terms = jnp.einsum('bts,btc->bsc', band, grads_ext)
        gated_grad = (back_terms[:block_count, filter_size:] + back_terms[1:, :filter_size]).reshape(token_count, per_group)
        filtered = convolved + bias_part[None, :] * signal_part
        output = (query_part * filtered).astype(jnp.bfloat16)
        grad_query = (cotangent_part * filtered).astype(jnp.bfloat16)
        gated_grad = gated_grad + bias_part[None, :] * grad_part
        grad_key = (gated_grad * value_part).astype(jnp.bfloat16)
        grad_value = (gated_grad * key_part).astype(jnp.bfloat16)
        bias_term = lax.optimization_barrier(jnp.sum(grad_part * signal_part, axis=0))
        products = jnp.einsum('btc,bsc->bts', grads_ext[:block_count], windows)
        products = jnp.where(visible[:block_count], products, jnp.zeros((), jnp.float32)).sum(axis=0)
        return (output, grad_query, grad_key, grad_value, fold_lags(products), bias_term)
    pieces = lax.map(one_group, jnp.arange(group_count, dtype=jnp.int32))

    def merge_groups(stacked):
        return jnp.transpose(stacked, (1, 0, 2)).reshape(token_count, channel_count)
    filter_scale = 1.0 / math.sqrt(token_count * per_group)
    bias_scale = 1.0 / math.sqrt(token_count)
    grad_filter = pieces[4] * filter_scale
    grad_bias = pieces[5].reshape(channel_count) * bias_scale
    return (merge_groups(pieces[0]), merge_groups(pieces[1]), merge_groups(pieces[2]), merge_groups(pieces[3]), grad_filter, grad_bias)
```

```python
import functools
import math

import jax
import jax.numpy as jnp
from jax import lax
from jax.experimental import pallas as pl
from jax.experimental.pallas import tpu as pltpu
from jax.sharding import PartitionSpec as P

F32, BF16 = jnp.float32, jnp.bfloat16
LANES = 128
TB = 16
WIDE = 256
X_CHUNKS = 1
DY_CHUNKS = 1


def lane_iota(shape):
    return lax.broadcasted_iota(jnp.int32, shape, len(shape) - 1)


def swap_chunks(arrays, chunk):
    count = len(arrays)
    pos = lane_iota(arrays[0].shape) // chunk
    turned = [pltpu.roll(a, n * chunk, 1) if n else a for n, a in enumerate(arrays)]
    rows = [turned[(-i) % count] for i in range(count)]
    bit = 1
    while bit < count:
        moved = (pos & bit) != 0
        rows = [jnp.where(moved, rows[(i - bit) % count], rows[i]) for i in range(count)]
        bit *= 2
    return [pltpu.roll(a, LANES - n * chunk, 1) if n else a for n, a in enumerate(rows)]


def to_groups(block, chunk):
    per = LANES // chunk
    sets = []
    for first in range(0, block.shape[0], TB * per):
        parts = [block[first + TB * n : first + TB * (n + 1)] for n in range(per)]
        sets.append(swap_chunks(parts, chunk))
    return [[s[g] for s in sets] for g in range(per)]


def windows(ext, chunk, count):
    per = LANES // chunk
    width = len(ext) - count // per
    out = []
    for i in range(count + 1):
        whole, part = divmod(i, per)
        if part == 0:
            vregs = ext[whole : whole + width]
        else:
            turned = [pltpu.roll(a, LANES - chunk * part, 1) for a in ext[whole : whole + width + 1]]
            keep = lane_iota(ext[0].shape) < LANES - chunk * part
            vregs = [jnp.where(keep, turned[v], turned[v + 1]) for v in range(width)]
        out.append(vregs[0] if width == 1 else jnp.concatenate(vregs, axis=1))
    return out


def side_by_side(vregs):
    return vregs[0] if len(vregs) == 1 else jnp.concatenate(vregs, axis=1)


def product_bf16(a, b):
    return (a.astype(F32) * b.astype(F32)).astype(BF16)


def from_groups(chunked, sub_groups, row_count, chunk):
    per = LANES // chunk
    rows = []
    for first in range(0, row_count // (TB * per)):
        parts = [chunked[g, :, first * LANES : (first + 1) * LANES] for g in range(sub_groups)]
        rows += swap_chunks(parts, chunk)
    return jnp.concatenate(rows, axis=0)


def skew_left(products):
    moved = pltpu.roll(products, WIDE - products.shape[0], 1, stride=1, stride_axis=0)
    return jnp.sum(moved, axis=0, keepdims=True)


def turned_rows(block):
    size = block.shape[0]
    ones = lax.broadcasted_iota(jnp.int32, (size, size), 0) + lane_iota((size, size)) == size - 1
    return jnp.dot(ones.astype(F32).astype(BF16), block, preferred_element_type=F32).astype(BF16)


def conv_kernel(chunk, filter_size, classes, q_ref, ct_ref, k_ref, v_ref, rim_ref, mask_ref, sel_ref, order_ref,
                taps_ref, bias_ref, *rest):
    out_ref, gq_ref, gf_ref, gb_ref, x_s, dy_s, conv_s, grad_s = rest[-8:]
    row_count, width = q_ref.shape
    per = LANES // chunk
    steps = filter_size // TB
    span = (steps + 1) * TB
    row = lax.broadcasted_iota(jnp.int32, (2 * TB, WIDE), 0)
    col = lane_iota((2 * TB, WIDE))
    band = ((row < TB) & (col < span)) | ((row >= TB) & (col >= span) & (col < span + TB))
    turned_band = ((row >= TB) & (col < span)) | ((row < TB) & (col >= span) & (col < span + TB))

    def one(sub, carry):
        lanes = pl.ds(pl.multiple_of(sub * LANES, LANES), LANES)
        x = product_bf16(k_ref[:, lanes], v_ref[:, lanes])
        dy = product_bf16(ct_ref[:, lanes], q_ref[:, lanes])
        gb_ref[:, lanes] = jnp.sum(x.astype(F32) * dy.astype(F32), axis=0, keepdims=True)
        xs, dys, rims = to_groups(x, chunk), to_groups(dy, chunk), to_groups(rim_ref[:, lanes], chunk)
        for g in range(per):
            xg, dyg = side_by_side(xs[g]), side_by_side(dys[g])
            x_s[g], dy_s[g] = xg, dyg
            window = jnp.concatenate(windows(rims[g] + xs[g], chunk, steps) + [xg], axis=0) * mask_ref[...]
            base = jnp.broadcast_to(taps_ref[pl.ds(sub * per + g, 1), :], (2 * TB, WIDE))
            taps = jnp.where(band, pltpu.roll(base, 0, 1, stride=1, stride_axis=0), 0.0).astype(BF16)
            y = jnp.dot(taps[:, : span + TB], window, preferred_element_type=F32)
            conv_s[g] = y[:TB] * sel_ref[:TB, :] + y[TB:] * sel_ref[TB:, :]
            dy2 = jnp.concatenate([dyg, dyg], axis=0) * mask_ref[span - TB : span + TB, :]
            pairs = lax.dot_general(turned_rows(dy2), window, (((1,), (1,)), ((), ())), preferred_element_type=F32)
            pairs = jnp.concatenate([pairs, jnp.zeros((2 * TB, WIDE - span - TB), F32)], axis=1)
            grad_s[g : g + 1, :] = skew_left(jnp.where(turned_band, pairs, 0.0))

        def more(index, carry):
            level, g = index // per, index % per
            here = order_ref[...] == level.astype(F32)
            xq = jnp.where(here, x_s[g].astype(F32), 0.0).astype(BF16)
            dyq = jnp.where(here, dy_s[g].astype(F32), 0.0).astype(BF16)
            base = jnp.broadcast_to(taps_ref[pl.ds(sub * per + g, 1), :], (TB, WIDE))
            taps = pltpu.roll(base, 0, 1, stride=1, stride_axis=0).astype(BF16)
            y = jnp.dot(taps[:, filter_size : filter_size + TB], xq, preferred_element_type=F32)
            conv_s[g] += jnp.where(here, y, 0.0)
            pairs = lax.dot_general(turned_rows(dyq), xq, (((1,), (1,)), ((), ())), preferred_element_type=F32)
            pairs = jnp.concatenate(
                [jnp.zeros((TB, filter_size), F32), pairs, jnp.zeros((TB, WIDE - filter_size - TB), F32)], axis=1
            )
            grad_s[pl.ds(g, 1), :] += skew_left(pairs)
            return carry

        lax.fori_loop(2 * per, classes[0] * per, more, 0)
        first = pl.multiple_of(sub * per, per)
        gf_ref[pl.ds(first, per), :] = grad_s[:, :filter_size]
        conv = from_groups(conv_s, per, row_count, chunk)
        filtered = conv + bias_ref[:, lanes] * x.astype(F32)
        out_ref[:, lanes] = (q_ref[:, lanes].astype(F32) * filtered).astype(BF16)
        gq_ref[:, lanes] = (ct_ref[:, lanes].astype(F32) * filtered).astype(BF16)
        return carry

    lax.fori_loop(0, width // LANES, one, 0)


def back_kernel(chunk, filter_size, classes, q_ref, ct_ref, k_ref, v_ref, rim_ref, mask_ref, sel_ref, order_ref,
                taps_ref, bias_ref, *rest):
    gk_ref, gv_ref, dy_s, back_s = rest[-4:]
    row_count, width = q_ref.shape
    per = LANES // chunk
    steps = filter_size // TB
    span = (steps + 1) * TB
    row = lax.broadcasted_iota(jnp.int32, (2 * TB, WIDE), 0)
    col = lane_iota((2 * TB, WIDE))
    band = (row >= TB) | (col < TB)

    def one(sub, carry):
        lanes = pl.ds(pl.multiple_of(sub * LANES, LANES), LANES)
        dy = product_bf16(ct_ref[:, lanes], q_ref[:, lanes])
        dys, rims = to_groups(dy, chunk), to_groups(rim_ref[:, lanes], chunk)
        for g in range(per):
            dyg = side_by_side(dys[g])
            dy_s[g] = dyg
            window = jnp.concatenate([dyg] + windows(dys[g] + rims[g], chunk, steps), axis=0) * mask_ref[...]
            base = jnp.broadcast_to(taps_ref[pl.ds(sub * per + g, 1), :], (2 * TB, WIDE))
            taps = jnp.where(band, pltpu.roll(base, 0, 1, stride=1, stride_axis=0), 0.0).astype(BF16)
            y = jnp.dot(taps[:, : span + TB], window, preferred_element_type=F32)
            back_s[g] = y[:TB] * sel_ref[:TB, :] + y[TB:] * sel_ref[TB:, :]

        def more(index, carry):
            level, g = index // per, index % per
            here = order_ref[...] == level.astype(F32)
            dyq = jnp.where(here, dy_s[g].astype(F32), 0.0).astype(BF16)
            base = jnp.broadcast_to(taps_ref[pl.ds(sub * per + g, 1), :], (TB, WIDE))
            taps = pltpu.roll(base, 0, 1, stride=1, stride_axis=0).astype(BF16)
            y = jnp.dot(taps[:, :TB], dyq, preferred_element_type=F32)
            back_s[g] += jnp.where(here, y, 0.0)
            return carry

        lax.fori_loop(2 * per, classes[0] * per, more, 0)
        back = from_groups(back_s, per, row_count, chunk)
        back = back + bias_ref[:, lanes] * dy.astype(F32)
        gk_ref[:, lanes] = (back * v_ref[:, lanes].astype(F32)).astype(BF16)
        gv_ref[:, lanes] = (back * k_ref[:, lanes].astype(F32)).astype(BF16)
        return carry

    lax.fori_loop(0, width // LANES, one, 0)


def run_part(kernel, name, part, parts, classes, big, rim, masks, taps, bias, small, previous):
    row_count, channels = big[0].shape
    mask, sel, order = masks
    group_count, filter_size = taps.shape[0], rim.shape[0]
    chunk = channels // group_count
    width = channels // parts
    block = math.gcd(width, 512)
    groups = block // chunk
    count, first = width // block, part * (width // block)
    at = lambda i, c: (0, first + i)
    whole = lambda i, c: (0, 0)
    cols = lambda rows: pl.BlockSpec((rows, block), at)
    fixed = lambda a: pl.BlockSpec(a.shape, whole)
    in_specs = [cols(row_count)] * 4 + [pl.BlockSpec((rim.shape[0], block), lambda i, c: (0, i))]
    in_specs += [fixed(mask), fixed(sel), fixed(order)]
    in_specs += [pl.BlockSpec((groups, WIDE), lambda i, c: (first + i, 0)), cols(1)]
    out_shape = [jax.ShapeDtypeStruct((row_count, channels), BF16)] * 2
    out_specs = [cols(row_count)] * 2
    scratch = [pltpu.VMEM((LANES // chunk, TB, row_count), BF16)]
    if small:
        out_shape += [jax.ShapeDtypeStruct((group_count, filter_size), F32), jax.ShapeDtypeStruct((1, channels), F32)]
        out_specs += [pl.BlockSpec((groups, filter_size), lambda i, c: (first + i, 0)), cols(1)]
        scratch += [pltpu.VMEM((LANES // chunk, TB, row_count), BF16)]
    scratch += [pltpu.VMEM((LANES // chunk, TB, row_count), F32)]
    if small:
        scratch += [pltpu.VMEM((LANES // chunk, WIDE), F32)]
    operands = [*big, rim, mask, sel, order, taps, bias]
    aliases = {}
    if previous is not None:
        aliases = {1 + len(operands) + i: i for i in range(len(previous))}
        in_specs += [pl.BlockSpec(memory_space=pl.ANY)] * len(previous)
        operands += list(previous)
    return pl.pallas_call(
        functools.partial(kernel, chunk, filter_size),
        grid_spec=pltpu.PrefetchScalarGridSpec(
            num_scalar_prefetch=1, grid=(count,), in_specs=in_specs, out_specs=out_specs, scratch_shapes=scratch
        ),
        out_shape=out_shape,
        input_output_aliases=aliases,
        compiler_params=pltpu.CompilerParams(vmem_limit_bytes=48 * 1024 * 1024),
        cost_estimate=pl.CostEstimate(
            flops=2 * row_count * width * 512, bytes_accessed=12 * row_count * width, transcendentals=0
        ),
        name=name,
    )(classes, *operands)


def reset_masks(starts, base, row_count, steps, chunk):
    blocks = row_count // TB
    near = lax.dynamic_slice_in_dim(starts, base, row_count + steps * TB, 0) - base
    ahead = near.reshape(blocks + steps, TB)
    own = ahead[:blocks]
    pos = jnp.arange(row_count, dtype=jnp.int32).reshape(blocks, TB)
    begins = (own == pos) & (jnp.arange(TB) > 0)[None, :]
    order = jnp.cumsum(begins.astype(jnp.int32), axis=1)
    behind = order[:, -1:] - order
    back = jnp.arange(steps, 0, -1, dtype=jnp.int32)[:, None, None]
    seen = [(pos[None] - TB * back) >= own[None, :, :1], (order == 0)[None], (order == 1)[None]]
    mask_x = jnp.concatenate(seen, axis=0)
    later = jnp.stack([ahead[m : m + blocks] for m in range(1, steps + 1)])
    kept = [(behind == 1)[None], (behind == 0)[None], later <= pos[None, :, -1:]]
    mask_dy = jnp.concatenate(kept, axis=0)

    def laid_out(a, kind):
        rows = a.shape[0] * TB
        flat = jnp.transpose(a, (0, 2, 1)).reshape(rows, blocks).astype(kind)
        return jnp.broadcast_to(flat[:, :, None], (rows, blocks, chunk)).reshape(rows, row_count)

    masks_x = (laid_out(mask_x, BF16), laid_out(mask_x[steps:], F32), laid_out(order[None], F32))
    masks_dy = (laid_out(mask_dy, BF16), laid_out(mask_dy[:2], F32), laid_out(behind[None], F32))
    classes = (1 + jnp.max(order)).reshape(1)
    return classes, masks_x, masks_dy


def passed_along(value, axis, steps):
    count = lax.axis_size(axis)
    initial, last = (max(0, -steps), min(count, count - steps))
    return lax.ppermute(value, axis, [(source, source + steps) for source in range(initial, last)])


def sum_over(value, axis):
    count = lax.axis_size(axis)
    if count & (count - 1):
        return lax.psum(value, axis)
    step = 1
    while step < count:
        value = value + lax.ppermute(value, axis, [(i, i ^ step) for i in range(count)])
        step *= 2
    return value


def rows_of_all(value, axis):
    count = lax.axis_size(axis)
    if count != 2:
        return lax.all_gather(value, axis, axis=0, tiled=True)
    other = lax.ppermute(value, axis, [(0, 1), (1, 0)])
    is_first = lax.axis_index(axis) == 0
    return jnp.concatenate([jnp.where(is_first, value, other), jnp.where(is_first, other, value)], axis=0)


def body(queries, key_branch, value_branch, cotangent, filters, skip_bias, contig_start):
    row_count, channels = queries.shape
    group_total, filter_size = filters.shape
    ctx_count, tp_count = lax.axis_size("ctx"), lax.axis_size("tp")
    shard, tensor = lax.axis_index("ctx"), lax.axis_index("tp")
    token_count = row_count * ctx_count
    chunk = channels * tp_count // group_total
    groups = channels // chunk
    steps = filter_size // TB

    def rims(a, b, first, direction, parts):
        width = channels // parts
        sent = []
        for part in range(parts):
            cut = lambda m: lax.slice(m, (first, part * width), (first + filter_size, (part + 1) * width))
            sent.append(passed_along(product_bf16(cut(a), cut(b)), "ctx", direction))
        return sent

    left = rims(key_branch, value_branch, row_count - filter_size, 1, X_CHUNKS)
    right = rims(cotangent, queries, 0, -1, DY_CHUNKS)

    starts = jnp.concatenate([contig_start, jnp.full((filter_size,), 2**30, jnp.int32)])
    classes, masks_x, masks_dy = reset_masks(starts, shard * row_count, row_count, steps, chunk)
    taps = lax.dynamic_slice_in_dim(filters, tensor * groups, groups, 0)
    taps_x = jnp.pad(taps[:, ::-1], ((0, 0), (1, WIDE - filter_size - 1)))
    taps_dy = jnp.pad(taps, ((0, 0), (0, WIDE - filter_size)))
    bias = skip_bias.reshape(1, channels)
    big = (queries, cotangent, key_branch, value_branch)

    done = None
    for part in range(X_CHUNKS):
        done = run_part(conv_kernel, "conv", part, X_CHUNKS, classes, big, left[part], masks_x, taps_x, bias, True, done)
    output, grad_query, filter_part, bias_part = done
    done = None
    for part in range(DY_CHUNKS):
        done = run_part(back_kernel, "back", part, DY_CHUNKS, classes, big, right[part], masks_dy, taps_dy, bias, False, done)
    grad_key, grad_value = done

    terms = jnp.concatenate([filter_part, bias_part.reshape(channels // filter_size, filter_size)], axis=0)
    terms = sum_over(terms, "ctx")
    filter_sum = rows_of_all(terms[:groups], "tp")
    grad_filter = filter_sum[:, ::-1] * (1.0 / math.sqrt(token_count * chunk))
    grad_bias = terms[groups:].reshape(channels) * (1.0 / math.sqrt(token_count))
    return (output, grad_query, grad_key, grad_value, grad_filter, grad_bias)


def solution(mesh):
    wide = P("ctx", "tp")
    return jax.shard_map(
        body,
        mesh=mesh,
        in_specs=(wide, wide, wide, wide, P(), P("tp"), P()),
        out_specs=(wide, wide, wide, wide, P(), P("tp")),
        check_vma=False,
    )
```

```python
import functools
import math

import jax
import jax.numpy as jnp
from jax import lax
from jax.experimental import pallas as pl
from jax.experimental.pallas import tpu as pltpu
from jax.sharding import PartitionSpec as P

F32, BF16 = jnp.float32, jnp.bfloat16
LANES = 128
TB = 16
WIDE = 256
KINDS = 3
PARTS = 4
IN_FLIGHT = 2


def iota(shape, axis):
    return lax.broadcasted_iota(jnp.int32, shape, axis)


def flag(condition, kind=BF16):
    return jnp.where(condition, 1.0, 0.0).astype(kind)


def permutation(size):
    return flag(iota((size, size), 0) + iota((size, size), 1) == size - 1)


def chunk_of(shape, kind, chunk):
    return (iota(shape, 1) // chunk).astype(F32).astype(kind)


def swap_chunks(arrays, bits, chunk):
    count = len(arrays)
    turned = [pltpu.roll(a, n * chunk, 1) if n else a for n, a in enumerate(arrays)]
    rows = [turned[(-i) % count] for i in range(count)]
    for power, moved in enumerate(bits):
        bit = 1 << power
        rows = [jnp.where(moved, rows[(i - bit) % count], rows[i]) for i in range(count)]
    return [pltpu.roll(a, LANES - n * chunk, 1) if n else a for n, a in enumerate(rows)]


def chunk_bits(kind, chunk):
    pos = iota((TB, LANES), 1) // chunk
    return [flag((pos >> power) & 1 == 1, kind) > 0 for power in range((LANES // chunk).bit_length() - 1)]


def to_groups(block, bits, chunk):
    per = LANES // chunk
    sets = []
    for first in range(0, block.shape[0], TB * per):
        parts = [block[first + TB * n : first + TB * (n + 1)] for n in range(per)]
        sets.append(swap_chunks(parts, bits, chunk))
    return [[s[g] for s in sets] for g in range(per)]


def from_groups(chunked, bits, chunk):
    rows = []
    for first in range(0, chunked[0].shape[1], LANES):
        rows += swap_chunks([a[:, first : first + LANES] for a in chunked], bits, chunk)
    return jnp.concatenate(rows, axis=0)


def windows(ext, pos, chunk, count):
    per = LANES // chunk
    width = len(ext) - count // per
    out = []
    for i in range(count + 1):
        whole, part = divmod(i, per)
        if part == 0:
            vregs = ext[whole : whole + width]
        else:
            turned = [pltpu.roll(a, LANES - chunk * part, 1) for a in ext[whole : whole + width + 1]]
            vregs = [jnp.where(pos < per - part, turned[v], turned[v + 1]) for v in range(width)]
        out.append(side_by_side(vregs))
    return out


def side_by_side(vregs):
    return vregs[0] if len(vregs) == 1 else jnp.concatenate(vregs, axis=1)


def product_bf16(a, b):
    return (a.astype(F32) * b.astype(F32)).astype(BF16)


def skew_left(products):
    moved = pltpu.roll(products, WIDE - products.shape[0], 1, stride=1, stride_axis=0)
    return jnp.sum(moved, axis=0, keepdims=True)


def shifted_taps(row, first):
    base = jnp.concatenate([row, jnp.zeros((1, WIDE - row.shape[1]), F32)], axis=1)
    base = jnp.broadcast_to(base, (TB, WIDE))
    return pltpu.roll(base, first, 1, stride=1, stride_axis=0).astype(BF16)


def with_kinds(taps, own, chunk):
    pos = chunk_of((TB, LANES), BF16, chunk)
    zero = jnp.zeros((TB, LANES), BF16)
    rows = [taps]
    for kind in range(1, KINDS):
        rows.append(jnp.concatenate([zero, jnp.where(pos == kind, pltpu.roll(own, kind * TB, 1), zero)], axis=1))
    return jnp.concatenate(rows, axis=0)


def chosen(products, sel_ref):
    return sum(products[kind * TB : (kind + 1) * TB] * sel_ref[kind * TB : (kind + 1) * TB, :] for kind in range(KINDS))


def conv_kernel(chunk, info, q_ref, ct_ref, k_ref, v_ref, rim_ref, mask_ref, turned_ref, sel_ref, order_ref,
                taps_ref, bias_ref, *rest):
    out_ref, gq_ref, gf_ref, gb_ref, x_s, dy_s, conv_s, grad_s = rest[-8:]
    row_count, width = q_ref.shape
    filter_size = taps_ref.shape[1]
    per = LANES // chunk
    steps = filter_size // TB
    span = (steps + 1) * TB
    depth = span + (KINDS - 1) * TB

    def one(sub, further):
        lanes = pl.ds(pl.multiple_of(sub * LANES, LANES), LANES)
        slot = 0
        bits, bits32 = chunk_bits(BF16, chunk), chunk_bits(F32, chunk)
        pos = chunk_of((TB, LANES), BF16, chunk)
        kind = KINDS - 1 - iota((KINDS * TB, WIDE), 0) // TB
        col = iota((KINDS * TB, WIDE), 1) - (kind + 1) * TB
        band = (col < filter_size) & ((kind == 0) | (col >= filter_size - TB))
        x = product_bf16(k_ref[:, lanes], v_ref[:, lanes])
        dy = product_bf16(ct_ref[:, lanes], q_ref[:, lanes])
        gb_ref[:, lanes] = jnp.sum(x.astype(F32) * dy.astype(F32), axis=0, keepdims=True)
        xs, dys = to_groups(x, bits, chunk), to_groups(dy, bits, chunk)
        rims = to_groups(rim_ref[:, lanes], bits, chunk)
        taps = taps_ref[pl.ds(pl.multiple_of(sub * per, per), per), :].astype(BF16)
        taps = jnp.dot(taps, permutation(filter_size), preferred_element_type=F32)
        for g in range(per):
            xg, dyg = side_by_side(xs[g]), side_by_side(dys[g])
            if further:
                x_s[slot, g], dy_s[slot, g] = xg, dyg
            window = windows(rims[g] + xs[g], pos, chunk, steps) + [xg] * (KINDS - 1)
            window = jnp.concatenate(window, axis=0) * mask_ref[...]
            band_taps = shifted_taps(taps[g : g + 1], 1)
            band_taps = with_kinds(band_taps, band_taps[:, LANES:], chunk)
            conv_s[slot, g] = chosen(jnp.dot(band_taps[:, :depth], window, preferred_element_type=F32), sel_ref)
            turned = jnp.dot(permutation(TB), dyg, preferred_element_type=F32).astype(BF16)
            turned = jnp.concatenate([turned] * KINDS, axis=0) * turned_ref[...]
            pairs = lax.dot_general(turned, window, (((1,), (1,)), ((), ())), preferred_element_type=F32)
            pairs = jnp.concatenate([pairs, jnp.zeros((KINDS * TB, WIDE - depth), F32)], axis=1)
            grad_s[slot, g : g + 1, :] = skew_left(jnp.where(band, pairs, 0.0))

        def more(index, carry):
            level, g = index // per, index % per
            here = order_ref[...] == level.astype(F32)
            xq = jnp.where(here, x_s[slot, g].astype(F32), 0.0).astype(BF16)
            dyq = jnp.where(here, dy_s[slot, g].astype(F32), 0.0).astype(BF16)
            row = taps_ref[pl.ds(sub * per + g, 1), :].astype(BF16)
            row = jnp.dot(row, permutation(filter_size), preferred_element_type=F32)
            own = shifted_taps(row, 1)[:, filter_size : filter_size + TB]
            conv_s[slot, g] += jnp.where(here, jnp.dot(own, xq, preferred_element_type=F32), 0.0)
            turned = jnp.dot(permutation(TB), dyq, preferred_element_type=F32).astype(BF16)
            pairs = lax.dot_general(turned, xq, (((1,), (1,)), ((), ())), preferred_element_type=F32)
            pairs = jnp.concatenate(
                [jnp.zeros((TB, filter_size), F32), pairs, jnp.zeros((TB, WIDE - filter_size - TB), F32)], axis=1
            )
            grad_s[slot, pl.ds(g, 1), :] += skew_left(pairs)
            return carry

        if further:
            lax.fori_loop(KINDS * per, info[0] * per, more, 0)
        gf_ref[pl.ds(pl.multiple_of(sub * per, per), per), :] = jnp.dot(
            grad_s[slot, :, :filter_size],
            permutation(filter_size).astype(F32),
            precision=lax.Precision.HIGHEST,
            preferred_element_type=F32,
        )
        conv = from_groups([conv_s[slot, g] for g in range(per)], bits32, chunk)
        filtered = conv + bias_ref[:, lanes] * x.astype(F32)
        out_ref[:, lanes] = (q_ref[:, lanes].astype(F32) * filtered).astype(BF16)
        gq_ref[:, lanes] = (ct_ref[:, lanes].astype(F32) * filtered).astype(BF16)

    for_all_lanes(one, width // LANES, info)


def back_kernel(chunk, info, q_ref, ct_ref, k_ref, v_ref, rim_ref, mask_ref, sel_ref, order_ref,
                taps_ref, bias_ref, *rest):
    gk_ref, gv_ref, dy_s, back_s = rest[-4:]
    row_count, width = q_ref.shape
    filter_size = taps_ref.shape[1]
    per = LANES // chunk
    steps = filter_size // TB
    depth = (steps + KINDS) * TB

    def one(sub, further):
        lanes = pl.ds(pl.multiple_of(sub * LANES, LANES), LANES)
        slot = 0
        bits, bits32 = chunk_bits(BF16, chunk), chunk_bits(F32, chunk)
        pos = chunk_of((TB, LANES), BF16, chunk)
        dy = product_bf16(ct_ref[:, lanes], q_ref[:, lanes])
        dys, rims = to_groups(dy, bits, chunk), to_groups(rim_ref[:, lanes], bits, chunk)
        taps = taps_ref[pl.ds(pl.multiple_of(sub * per, per), per), :]
        for g in range(per):
            dyg = side_by_side(dys[g])
            if further:
                dy_s[slot, g] = dyg
            window = windows(dys[g] + rims[g], pos, chunk, steps) + [dyg] * (KINDS - 1)
            window = jnp.concatenate(window, axis=0) * mask_ref[...]
            band_taps = shifted_taps(taps[g : g + 1], 0)
            band_taps = with_kinds(band_taps, band_taps[:, :LANES], chunk)
            back_s[slot, g] = chosen(jnp.dot(band_taps[:, :depth], window, preferred_element_type=F32), sel_ref)

        def more(index, carry):
            level, g = index // per, index % per
            here = order_ref[...] == level.astype(F32)
            dyq = jnp.where(here, dy_s[slot, g].astype(F32), 0.0).astype(BF16)
            own = shifted_taps(taps_ref[pl.ds(sub * per + g, 1), :], 0)[:, :TB]
            back_s[slot, g] += jnp.where(here, jnp.dot(own, dyq, preferred_element_type=F32), 0.0)
            return carry

        if further:
            lax.fori_loop(KINDS * per, info[0] * per, more, 0)
        back = from_groups([back_s[slot, g] for g in range(per)], bits32, chunk)
        back = back + bias_ref[:, lanes] * dy.astype(F32)
        gk_ref[:, lanes] = (back * v_ref[:, lanes].astype(F32)).astype(BF16)
        gv_ref[:, lanes] = (back * k_ref[:, lanes].astype(F32)).astype(BF16)

    for_all_lanes(one, width // LANES, info)


def for_all_lanes(one, count, info):
    def run(further):
        def step(sub, carry):
            one(sub, further)
            return carry

        lax.fori_loop(0, count, step, 0)

    pl.when(info[0] <= KINDS)(lambda: run(False))
    pl.when(info[0] > KINDS)(lambda: run(True))


def run_part(kernel, name, part, info, big, rim, masks, filters, bias, small, previous):
    row_count, channels = big[0].shape
    filter_size = filters.shape[1]
    chunk = TB
    width = channels // PARTS
    block = math.gcd(width, 512)
    groups = block // chunk
    count, first = width // block, part * (width // block)
    cols = lambda rows: pl.BlockSpec((rows, block), lambda i, c: (0, first + i))
    in_specs = [cols(row_count)] * 4 + [pl.BlockSpec((rim.shape[0], block), lambda i, c: (0, i))]
    in_specs += [pl.BlockSpec(a.shape, lambda i, c: (0, 0)) for a in masks]
    taps_at = lambda i, c: (c[1] * (channels // block) + first + i, 0)
    in_specs += [pl.BlockSpec((groups, filter_size), taps_at), cols(1)]
    out_shape = [jax.ShapeDtypeStruct((row_count, channels), BF16)] * 2
    out_specs = [cols(row_count)] * 2
    slots, per = 1, LANES // chunk
    scratch = [pltpu.VMEM((slots, per, TB, row_count), BF16)] * (2 if small else 1)
    scratch += [pltpu.VMEM((slots, per, TB, row_count), F32)]
    if small:
        out_shape += [jax.ShapeDtypeStruct((channels // chunk, filter_size), F32), jax.ShapeDtypeStruct((1, channels), F32)]
        out_specs += [pl.BlockSpec((groups, filter_size), lambda i, c: (first + i, 0)), cols(1)]
        scratch += [pltpu.VMEM((slots, per, WIDE), F32)]
    operands = [*big, rim, *masks, filters, bias]
    aliases = {}
    if previous is not None:
        aliases = {1 + len(operands) + i: i for i in range(len(previous))}
        in_specs += [pl.BlockSpec(memory_space=pl.ANY)] * len(previous)
        operands += list(previous)
    return pl.pallas_call(
        functools.partial(kernel, chunk),
        grid_spec=pltpu.PrefetchScalarGridSpec(
            num_scalar_prefetch=1, grid=(count,), in_specs=in_specs, out_specs=out_specs, scratch_shapes=scratch
        ),
        out_shape=out_shape,
        input_output_aliases=aliases,
        compiler_params=pltpu.CompilerParams(vmem_limit_bytes=48 * 1024 * 1024),
        cost_estimate=pl.CostEstimate(flops=row_count * width, bytes_accessed=row_count * width, transcendentals=0),
        name=name,
    )(info, *operands)


def reset_kernel(steps, near_ref, mask_x, turned_x, sel_x, order_x, mask_dy, sel_dy, order_dy, kinds):
    total = near_ref.shape[1]
    rows = total - steps * TB
    near = jnp.clip(near_ref[...], -1024, 1024).astype(F32)
    lane, row = iota((TB, total), 1), iota((TB, total), 0)
    spread = jnp.where(lane % TB == row, jnp.broadcast_to(near, (TB, total)), 0.0)
    same = flag(iota((total, total), 0) // TB == iota((total, total), 1) // TB, F32)
    begin = jnp.dot(spread, same, precision=lax.Precision.HIGHEST, preferred_element_type=F32)
    begin = jnp.floor(begin + 0.5)
    own = begin[:, :rows]
    block = iota((TB, rows), 1) // TB * TB
    pos = (block + iota((TB, rows), 0)).astype(F32)
    marks = flag((own == pos) & (iota((TB, rows), 0) > 0))
    before = flag(iota((TB, TB), 0) >= iota((TB, TB), 1))
    order = jnp.dot(before, marks, preferred_element_type=F32)
    behind = order[TB - 1 :] - order
    first = jnp.broadcast_to(own[:1], (TB, rows))
    for i in range(steps):
        mask_x[i * TB : (i + 1) * TB, :] = flag(pos - TB * (steps - i) >= first)
        later = pltpu.roll(begin, total - (i + 1) * TB, 1)[:, :rows]
        mask_dy[(i + 1) * TB : (i + 2) * TB, :] = flag(later <= (block + TB - 1).astype(F32))
    turn = permutation(TB)
    for kind in range(KINDS):
        at = steps + kind
        mask_x[at * TB : (at + 1) * TB, :] = flag(order == kind)
        sel_x[kind * TB : (kind + 1) * TB, :] = flag(order == kind, F32)
        at = KINDS - 1 - kind
        turned = jnp.dot(turn, flag(order == kind), preferred_element_type=F32)
        turned_x[at * TB : (at + 1) * TB, :] = turned.astype(BF16)
        at = steps + kind if kind else 0
        mask_dy[at * TB : (at + 1) * TB, :] = flag(behind == kind)
        sel_dy[kind * TB : (kind + 1) * TB, :] = flag(behind == kind, F32)
    order_x[...], order_dy[...] = order, behind
    kinds[0] = 1 + jnp.max(order).astype(jnp.int32)


def reset_masks(near, row_count, steps):
    depth, high = (steps + KINDS) * TB, KINDS * TB
    shapes = [(depth, BF16), (high, BF16), (high, F32), (TB, F32), (depth, BF16), (high, F32), (TB, F32)]
    out = pl.pallas_call(
        functools.partial(reset_kernel, steps),
        out_shape=[jax.ShapeDtypeStruct((rows, row_count), kind) for rows, kind in shapes]
        + [jax.ShapeDtypeStruct((1,), jnp.int32)],
        out_specs=[pl.BlockSpec(memory_space=pltpu.VMEM)] * len(shapes) + [pl.BlockSpec(memory_space=pltpu.SMEM)],
        compiler_params=pltpu.CompilerParams(vmem_limit_bytes=32 * 1024 * 1024),
        name="resets",
    )(near)
    return out[:4], out[4:7], out[7]


def passed_along(value, axis, steps):
    count = lax.axis_size(axis)
    initial, last = (max(0, -steps), min(count, count - steps))
    return lax.ppermute(value, axis, [(source, source + steps) for source in range(initial, last)])


def sum_over(value, axis):
    count = lax.axis_size(axis)
    if count & (count - 1):
        return lax.psum(value, axis)
    step = 1
    while step < count:
        value = value + lax.ppermute(value, axis, [(i, i ^ step) for i in range(count)])
        step *= 2
    return value


def rows_of_all(value, axis):
    count = lax.axis_size(axis)
    if count != 2:
        return lax.all_gather(value, axis, axis=0, tiled=True)
    other = lax.ppermute(value, axis, [(0, 1), (1, 0)])
    is_first = lax.axis_index(axis) == 0
    return jnp.concatenate([jnp.where(is_first, value, other), jnp.where(is_first, other, value)], axis=0)


def body(queries, key_branch, value_branch, cotangent, filters, skip_bias, contig_start):
    row_count, channels = queries.shape
    group_total, filter_size = filters.shape
    ctx_count, tp_count = lax.axis_size("ctx"), lax.axis_size("tp")
    shard, tensor = lax.axis_index("ctx"), lax.axis_index("tp")
    token_count = row_count * ctx_count
    chunk = channels * tp_count // group_total
    groups = channels // chunk
    width = channels // PARTS

    def rim(a, b, first, part):
        cut = lambda m: lax.slice(m, (first, part * width), (first + filter_size, (part + 1) * width))
        return product_bf16(cut(a), cut(b))

    sends = [(rim(key_branch, value_branch, row_count - filter_size, part), 1) for part in range(PARTS)]
    sends += [(rim(cotangent, queries, 0, part), -1) for part in range(PARTS)]
    halos = []
    for index, (sent, direction) in enumerate(sends):
        if index >= IN_FLIGHT:
            sent, halos[index - IN_FLIGHT] = lax.optimization_barrier((sent, halos[index - IN_FLIGHT]))
        halos.append(passed_along(sent, "ctx", direction))

    starts = jnp.concatenate([contig_start, jnp.full((filter_size,), 2**30, jnp.int32)])
    first = shard * row_count
    near = (lax.dynamic_slice_in_dim(starts, first, row_count + filter_size, 0) - first)[None, :]
    masks_x, masks_dy, kinds = reset_masks(near, row_count, filter_size // TB)
    info = jnp.concatenate([kinds, tensor.astype(jnp.int32).reshape(1)])
    bias = skip_bias.reshape(1, channels)
    big = (queries, cotangent, key_branch, value_branch)

    done = None
    for part in range(PARTS):
        done = run_part(conv_kernel, "conv", part, info, big, halos[part], masks_x, filters, bias, True, done)
    output, grad_query, filter_part, bias_part = done
    done = None
    for part in range(PARTS):
        done = run_part(back_kernel, "back", part, info, big, halos[PARTS + part], masks_dy, filters, bias, False, done)
    grad_key, grad_value = done

    terms = jnp.concatenate([filter_part, bias_part.reshape(channels // filter_size, filter_size)], axis=0)
    terms = sum_over(terms, "ctx")
    grad_filter = rows_of_all(terms[:groups], "tp") * (1.0 / math.sqrt(token_count * chunk))
    grad_bias = terms[groups:].reshape(channels) * (1.0 / math.sqrt(token_count))
    return (output, grad_query, grad_key, grad_value, grad_filter, grad_bias)


def solution(mesh):
    wide = P("ctx", "tp")
    return jax.shard_map(
        body,
        mesh=mesh,
        in_specs=(wide, wide, wide, wide, P(), P("tp"), P()),
        out_specs=(wide, wide, wide, wide, P(), P("tp")),
        check_vma=False,
    )
```

```python
import functools
import math

import jax
import jax.numpy as jnp
from jax import lax
from jax.experimental import pallas as pl
from jax.experimental.pallas import tpu as pltpu
from jax.sharding import PartitionSpec as P

F32, BF16 = jnp.float32, jnp.bfloat16
LANES = 128
TB = 16
WIDE = 256
KINDS = 3
PARTS = 2
IN_FLIGHT = 2


def iota(shape, axis):
    return lax.broadcasted_iota(jnp.int32, shape, axis)


def flag(condition, kind=BF16):
    return jnp.where(condition, 1.0, 0.0).astype(kind)


def permutation(size):
    return flag(iota((size, size), 0) + iota((size, size), 1) == size - 1)


def chunk_of(shape, kind, chunk):
    return (iota(shape, 1) // chunk).astype(F32).astype(kind)


def swap_chunks(arrays, bits, chunk):
    count = len(arrays)
    turned = [pltpu.roll(a, n * chunk, 1) if n else a for n, a in enumerate(arrays)]
    rows = [turned[(-i) % count] for i in range(count)]
    for power, moved in enumerate(bits):
        bit = 1 << power
        rows = [jnp.where(moved, rows[(i - bit) % count], rows[i]) for i in range(count)]
    return [pltpu.roll(a, LANES - n * chunk, 1) if n else a for n, a in enumerate(rows)]


def chunk_bits(kind, chunk):
    pos = iota((TB, LANES), 1) // chunk
    return [flag((pos >> power) & 1 == 1, kind) > 0 for power in range((LANES // chunk).bit_length() - 1)]


def to_groups(block, bits, chunk):
    per = LANES // chunk
    sets = []
    for first in range(0, block.shape[0], TB * per):
        parts = [block[first + TB * n : first + TB * (n + 1)] for n in range(per)]
        sets.append(swap_chunks(parts, bits, chunk))
    return [[s[g] for s in sets] for g in range(per)]


def from_groups(chunked, bits, chunk):
    rows = []
    for first in range(0, chunked[0].shape[1], LANES):
        rows += swap_chunks([a[:, first : first + LANES] for a in chunked], bits, chunk)
    return jnp.concatenate(rows, axis=0)


def windows(ext, pos, chunk, count):
    per = LANES // chunk
    width = len(ext) - count // per
    out = []
    for i in range(count + 1):
        whole, part = divmod(i, per)
        if part == 0:
            vregs = ext[whole : whole + width]
        else:
            turned = [pltpu.roll(a, LANES - chunk * part, 1) for a in ext[whole : whole + width + 1]]
            vregs = [jnp.where(pos < per - part, turned[v], turned[v + 1]) for v in range(width)]
        out.append(side_by_side(vregs))
    return out


def side_by_side(vregs):
    return vregs[0] if len(vregs) == 1 else jnp.concatenate(vregs, axis=1)


def product_bf16(a, b):
    return (a.astype(F32) * b.astype(F32)).astype(BF16)


def skew_left(products):
    moved = pltpu.roll(products, WIDE - products.shape[0], 1, stride=1, stride_axis=0)
    return jnp.sum(moved, axis=0, keepdims=True)


def shifted_taps(row, first):
    base = jnp.concatenate([row, jnp.zeros((1, WIDE - row.shape[1]), F32)], axis=1)
    base = jnp.broadcast_to(base, (TB, WIDE))
    return pltpu.roll(base, first, 1, stride=1, stride_axis=0).astype(BF16)


def with_kinds(taps, own, chunk):
    pos = chunk_of((TB, LANES), BF16, chunk)
    zero = jnp.zeros((TB, LANES), BF16)
    rows = [taps]
    for kind in range(1, KINDS):
        rows.append(jnp.concatenate([zero, jnp.where(pos == kind, pltpu.roll(own, kind * TB, 1), zero)], axis=1))
    return jnp.concatenate(rows, axis=0)


def both(one, two):
    rows, width = one[0].shape[0], one[1].shape[1]
    taps = jnp.concatenate([one[0], two[0]], axis=0)
    window = jnp.concatenate([one[1], two[1]], axis=1)
    y = jnp.dot(taps, window, preferred_element_type=F32)
    return y[:rows, :width], y[rows:, width:]


def chosen(products, sel_ref):
    return sum(products[kind * TB : (kind + 1) * TB] * sel_ref[kind * TB : (kind + 1) * TB, :] for kind in range(KINDS))


def conv_kernel(chunk, info, q_ref, ct_ref, k_ref, v_ref, rim_ref, mask_ref, turned_ref, sel_ref, order_ref,
                taps_ref, bias_ref, *rest):
    out_ref, gq_ref, gf_ref, gb_ref, x_s, dy_s, conv_s, grad_s = rest[-8:]
    row_count, width = q_ref.shape
    filter_size = taps_ref.shape[1]
    per = LANES // chunk
    steps = filter_size // TB
    span = (steps + 1) * TB
    depth = span + (KINDS - 1) * TB

    def one(sub, further):
        lanes = pl.ds(pl.multiple_of(sub * LANES, LANES), LANES)
        slot = 0
        bits, bits32 = chunk_bits(BF16, chunk), chunk_bits(F32, chunk)
        pos = chunk_of((TB, LANES), BF16, chunk)
        kind = KINDS - 1 - iota((KINDS * TB, WIDE), 0) // TB
        col = iota((KINDS * TB, WIDE), 1) - (kind + 1) * TB
        band = (col < filter_size) & ((kind == 0) | (col >= filter_size - TB))
        x = product_bf16(k_ref[:, lanes], v_ref[:, lanes])
        dy = product_bf16(ct_ref[:, lanes], q_ref[:, lanes])
        gb_ref[:, lanes] = jnp.sum(x.astype(F32) * dy.astype(F32), axis=0, keepdims=True)
        xs, dys = to_groups(x, bits, chunk), to_groups(dy, bits, chunk)
        rims = to_groups(rim_ref[:, lanes], bits, chunk)
        taps = taps_ref[pl.ds(pl.multiple_of(sub * per, per), per), :].astype(BF16)
        taps = jnp.dot(taps, permutation(filter_size), preferred_element_type=F32)
        pair = []
        for g in range(per):
            xg, dyg = side_by_side(xs[g]), side_by_side(dys[g])
            if further:
                x_s[slot, g], dy_s[slot, g] = xg, dyg
            window = windows(rims[g] + xs[g], pos, chunk, steps) + [xg] * (KINDS - 1)
            window = jnp.concatenate(window, axis=0) * mask_ref[...]
            band_taps = shifted_taps(taps[g : g + 1], 1)
            pair.append((with_kinds(band_taps, band_taps[:, LANES:], chunk)[:, :depth], window))
            if g % 2:
                conv_s[slot, g - 1], conv_s[slot, g] = [chosen(y, sel_ref) for y in both(*pair)]
                pair = []
            turned = jnp.dot(permutation(TB), dyg, preferred_element_type=F32).astype(BF16)
            turned = jnp.concatenate([turned] * KINDS, axis=0) * turned_ref[...]
            pairs = lax.dot_general(turned, window, (((1,), (1,)), ((), ())), preferred_element_type=F32)
            pairs = jnp.concatenate([pairs, jnp.zeros((KINDS * TB, WIDE - depth), F32)], axis=1)
            grad_s[slot, g : g + 1, :] = skew_left(jnp.where(band, pairs, 0.0))

        def more(index, carry):
            level, g = index // per, index % per
            here = order_ref[...] == level.astype(F32)
            xq = jnp.where(here, x_s[slot, g].astype(F32), 0.0).astype(BF16)
            dyq = jnp.where(here, dy_s[slot, g].astype(F32), 0.0).astype(BF16)
            row = taps_ref[pl.ds(sub * per + g, 1), :].astype(BF16)
            row = jnp.dot(row, permutation(filter_size), preferred_element_type=F32)
            own = shifted_taps(row, 1)[:, filter_size : filter_size + TB]
            conv_s[slot, g] += jnp.where(here, jnp.dot(own, xq, preferred_element_type=F32), 0.0)
            turned = jnp.dot(permutation(TB), dyq, preferred_element_type=F32).astype(BF16)
            pairs = lax.dot_general(turned, xq, (((1,), (1,)), ((), ())), preferred_element_type=F32)
            pairs = jnp.concatenate(
                [jnp.zeros((TB, filter_size), F32), pairs, jnp.zeros((TB, WIDE - filter_size - TB), F32)], axis=1
            )
            grad_s[slot, pl.ds(g, 1), :] += skew_left(pairs)
            return carry

        if further:
            lax.fori_loop(KINDS * per, info[0] * per, more, 0)
        gf_ref[pl.ds(pl.multiple_of(sub * per, per), per), :] = jnp.dot(
            grad_s[slot, :, :filter_size],
            permutation(filter_size).astype(F32),
            precision=lax.Precision.HIGHEST,
            preferred_element_type=F32,
        )
        conv = from_groups([conv_s[slot, g] for g in range(per)], bits32, chunk)
        filtered = conv + bias_ref[:, lanes] * x.astype(F32)
        out_ref[:, lanes] = (q_ref[:, lanes].astype(F32) * filtered).astype(BF16)
        gq_ref[:, lanes] = (ct_ref[:, lanes].astype(F32) * filtered).astype(BF16)

    for_all_lanes(one, width // LANES, info)


def back_kernel(chunk, info, q_ref, ct_ref, k_ref, v_ref, rim_ref, mask_ref, sel_ref, order_ref,
                taps_ref, bias_ref, *rest):
    gk_ref, gv_ref, dy_s, back_s = rest[-4:]
    row_count, width = q_ref.shape
    filter_size = taps_ref.shape[1]
    per = LANES // chunk
    steps = filter_size // TB
    depth = (steps + KINDS) * TB

    def one(sub, further):
        lanes = pl.ds(pl.multiple_of(sub * LANES, LANES), LANES)
        slot = 0
        bits, bits32 = chunk_bits(BF16, chunk), chunk_bits(F32, chunk)
        pos = chunk_of((TB, LANES), BF16, chunk)
        dy = product_bf16(ct_ref[:, lanes], q_ref[:, lanes])
        dys, rims = to_groups(dy, bits, chunk), to_groups(rim_ref[:, lanes], bits, chunk)
        taps = taps_ref[pl.ds(pl.multiple_of(sub * per, per), per), :]
        pair = []
        for g in range(per):
            dyg = side_by_side(dys[g])
            if further:
                dy_s[slot, g] = dyg
            window = windows(dys[g] + rims[g], pos, chunk, steps) + [dyg] * (KINDS - 1)
            window = jnp.concatenate(window, axis=0) * mask_ref[...]
            band_taps = shifted_taps(taps[g : g + 1], 0)
            pair.append((with_kinds(band_taps, band_taps[:, :LANES], chunk)[:, :depth], window))
            if g % 2:
                back_s[slot, g - 1], back_s[slot, g] = [chosen(y, sel_ref) for y in both(*pair)]
                pair = []

        def more(index, carry):
            level, g = index // per, index % per
            here = order_ref[...] == level.astype(F32)
            dyq = jnp.where(here, dy_s[slot, g].astype(F32), 0.0).astype(BF16)
            own = shifted_taps(taps_ref[pl.ds(sub * per + g, 1), :], 0)[:, :TB]
            back_s[slot, g] += jnp.where(here, jnp.dot(own, dyq, preferred_element_type=F32), 0.0)
            return carry

        if further:
            lax.fori_loop(KINDS * per, info[0] * per, more, 0)
        back = from_groups([back_s[slot, g] for g in range(per)], bits32, chunk)
        back = back + bias_ref[:, lanes] * dy.astype(F32)
        gk_ref[:, lanes] = (back * v_ref[:, lanes].astype(F32)).astype(BF16)
        gv_ref[:, lanes] = (back * k_ref[:, lanes].astype(F32)).astype(BF16)

    for_all_lanes(one, width // LANES, info)


def for_all_lanes(one, count, info):
    def run(further):
        def step(sub, carry):
            one(sub, further)
            return carry

        lax.fori_loop(0, count, step, 0)

    pl.when(info[0] <= KINDS)(lambda: run(False))
    pl.when(info[0] > KINDS)(lambda: run(True))


def run_part(kernel, name, part, info, big, rim, masks, filters, bias, small, previous):
    row_count, channels = big[0].shape
    filter_size = filters.shape[1]
    chunk = TB
    width = channels // PARTS
    block = math.gcd(width, 512)
    groups = block // chunk
    count, first = width // block, part * (width // block)
    cols = lambda rows: pl.BlockSpec((rows, block), lambda i, c: (0, first + i))
    in_specs = [cols(row_count)] * 4 + [pl.BlockSpec((rim.shape[0], block), lambda i, c: (0, i))]
    in_specs += [pl.BlockSpec(a.shape, lambda i, c: (0, 0)) for a in masks]
    taps_at = lambda i, c: (c[1] * (channels // block) + first + i, 0)
    in_specs += [pl.BlockSpec((groups, filter_size), taps_at), cols(1)]
    out_shape = [jax.ShapeDtypeStruct((row_count, channels), BF16)] * 2
    out_specs = [cols(row_count)] * 2
    slots, per = 1, LANES // chunk
    scratch = [pltpu.VMEM((slots, per, TB, row_count), BF16)] * (2 if small else 1)
    scratch += [pltpu.VMEM((slots, per, TB, row_count), F32)]
    if small:
        out_shape += [jax.ShapeDtypeStruct((channels // chunk, filter_size), F32), jax.ShapeDtypeStruct((1, channels), F32)]
        out_specs += [pl.BlockSpec((groups, filter_size), lambda i, c: (first + i, 0)), cols(1)]
        scratch += [pltpu.VMEM((slots, per, WIDE), F32)]
    operands = [*big, rim, *masks, filters, bias]
    aliases = {}
    if previous is not None:
        aliases = {1 + len(operands) + i: i for i in range(len(previous))}
        in_specs += [pl.BlockSpec(memory_space=pl.ANY)] * len(previous)
        operands += list(previous)
    return pl.pallas_call(
        functools.partial(kernel, chunk),
        grid_spec=pltpu.PrefetchScalarGridSpec(
            num_scalar_prefetch=1, grid=(count,), in_specs=in_specs, out_specs=out_specs, scratch_shapes=scratch
        ),
        out_shape=out_shape,
        input_output_aliases=aliases,
        compiler_params=pltpu.CompilerParams(vmem_limit_bytes=48 * 1024 * 1024),
        cost_estimate=pl.CostEstimate(flops=row_count * width, bytes_accessed=row_count * width, transcendentals=0),
        name=name,
    )(info, *operands)


def reset_kernel(steps, near_ref, mask_x, turned_x, sel_x, order_x, mask_dy, sel_dy, order_dy, kinds):
    total = near_ref.shape[1]
    rows = total - steps * TB
    near = jnp.clip(near_ref[...], -1024, 1024).astype(F32)
    lane, row = iota((TB, total), 1), iota((TB, total), 0)
    spread = jnp.where(lane % TB == row, jnp.broadcast_to(near, (TB, total)), 0.0)
    same = flag(iota((total, total), 0) // TB == iota((total, total), 1) // TB, F32)
    begin = jnp.dot(spread, same, precision=lax.Precision.HIGHEST, preferred_element_type=F32)
    begin = jnp.floor(begin + 0.5)
    own = begin[:, :rows]
    block = iota((TB, rows), 1) // TB * TB
    pos = (block + iota((TB, rows), 0)).astype(F32)
    marks = flag((own == pos) & (iota((TB, rows), 0) > 0))
    before = flag(iota((TB, TB), 0) >= iota((TB, TB), 1))
    order = jnp.dot(before, marks, preferred_element_type=F32)
    behind = order[TB - 1 :] - order
    first = jnp.broadcast_to(own[:1], (TB, rows))
    for i in range(steps):
        mask_x[i * TB : (i + 1) * TB, :] = flag(pos - TB * (steps - i) >= first)
        later = pltpu.roll(begin, total - (i + 1) * TB, 1)[:, :rows]
        mask_dy[(i + 1) * TB : (i + 2) * TB, :] = flag(later <= (block + TB - 1).astype(F32))
    turn = permutation(TB)
    for kind in range(KINDS):
        at = steps + kind
        mask_x[at * TB : (at + 1) * TB, :] = flag(order == kind)
        sel_x[kind * TB : (kind + 1) * TB, :] = flag(order == kind, F32)
        at = KINDS - 1 - kind
        turned = jnp.dot(turn, flag(order == kind), preferred_element_type=F32)
        turned_x[at * TB : (at + 1) * TB, :] = turned.astype(BF16)
        at = steps + kind if kind else 0
        mask_dy[at * TB : (at + 1) * TB, :] = flag(behind == kind)
        sel_dy[kind * TB : (kind + 1) * TB, :] = flag(behind == kind, F32)
    order_x[...], order_dy[...] = order, behind
    kinds[0] = 1 + jnp.max(order).astype(jnp.int32)


def reset_masks(near, row_count, steps):
    depth, high = (steps + KINDS) * TB, KINDS * TB
    shapes = [(depth, BF16), (high, BF16), (high, F32), (TB, F32), (depth, BF16), (high, F32), (TB, F32)]
    out = pl.pallas_call(
        functools.partial(reset_kernel, steps),
        out_shape=[jax.ShapeDtypeStruct((rows, row_count), kind) for rows, kind in shapes]
        + [jax.ShapeDtypeStruct((1,), jnp.int32)],
        out_specs=[pl.BlockSpec(memory_space=pltpu.VMEM)] * len(shapes) + [pl.BlockSpec(memory_space=pltpu.SMEM)],
        compiler_params=pltpu.CompilerParams(vmem_limit_bytes=32 * 1024 * 1024),
        name="resets",
    )(near)
    return out[:4], out[4:7], out[7]


def passed_along(value, axis, steps):
    count = lax.axis_size(axis)
    initial, last = (max(0, -steps), min(count, count - steps))
    return lax.ppermute(value, axis, [(source, source + steps) for source in range(initial, last)])


def sum_over(value, axis):
    count = lax.axis_size(axis)
    if count & (count - 1):
        return lax.psum(value, axis)
    step = 1
    while step < count:
        value = value + lax.ppermute(value, axis, [(i, i ^ step) for i in range(count)])
        step *= 2
    return value


def rows_of_all(value, axis):
    count = lax.axis_size(axis)
    if count != 2:
        return lax.all_gather(value, axis, axis=0, tiled=True)
    other = lax.ppermute(value, axis, [(0, 1), (1, 0)])
    is_first = lax.axis_index(axis) == 0
    return jnp.concatenate([jnp.where(is_first, value, other), jnp.where(is_first, other, value)], axis=0)


def body(queries, key_branch, value_branch, cotangent, filters, skip_bias, contig_start):
    row_count, channels = queries.shape
    group_total, filter_size = filters.shape
    ctx_count, tp_count = lax.axis_size("ctx"), lax.axis_size("tp")
    shard, tensor = lax.axis_index("ctx"), lax.axis_index("tp")
    token_count = row_count * ctx_count
    chunk = channels * tp_count // group_total
    groups = channels // chunk
    width = channels // PARTS

    def rim(a, b, first, part):
        cut = lambda m: lax.slice(m, (first, part * width), (first + filter_size, (part + 1) * width))
        return product_bf16(cut(a), cut(b))

    sends = [(rim(key_branch, value_branch, row_count - filter_size, part), 1) for part in range(PARTS)]
    sends += [(rim(cotangent, queries, 0, part), -1) for part in range(PARTS)]
    halos = []
    for index, (sent, direction) in enumerate(sends):
        if index >= IN_FLIGHT:
            sent, halos[index - IN_FLIGHT] = lax.optimization_barrier((sent, halos[index - IN_FLIGHT]))
        halos.append(passed_along(sent, "ctx", direction))

    starts = jnp.concatenate([contig_start, jnp.full((filter_size,), 2**30, jnp.int32)])
    first = shard * row_count
    near = (lax.dynamic_slice_in_dim(starts, first, row_count + filter_size, 0) - first)[None, :]
    masks_x, masks_dy, kinds = reset_masks(near, row_count, filter_size // TB)
    info = jnp.concatenate([kinds, tensor.astype(jnp.int32).reshape(1)])
    bias = skip_bias.reshape(1, channels)
    big = (queries, cotangent, key_branch, value_branch)

    done = None
    for part in range(PARTS):
        done = run_part(conv_kernel, "conv", part, info, big, halos[part], masks_x, filters, bias, True, done)
    output, grad_query, filter_part, bias_part = done
    done = None
    for part in range(PARTS):
        done = run_part(back_kernel, "back", part, info, big, halos[PARTS + part], masks_dy, filters, bias, False, done)
    grad_key, grad_value = done

    terms = jnp.concatenate([filter_part, bias_part.reshape(channels // filter_size, filter_size)], axis=0)
    terms = sum_over(terms, "ctx")
    grad_filter = rows_of_all(terms[:groups], "tp") * (1.0 / math.sqrt(token_count * chunk))
    grad_bias = terms[groups:].reshape(channels) * (1.0 / math.sqrt(token_count))
    return (output, grad_query, grad_key, grad_value, grad_filter, grad_bias)


def solution(mesh):
    wide = P("ctx", "tp")
    return jax.shard_map(
        body,
        mesh=mesh,
        in_specs=(wide, wide, wide, wide, P(), P("tp"), P()),
        out_specs=(wide, wide, wide, wide, P(), P("tp")),
        check_vma=False,
    )
```

```python
import functools
import math

import jax
import jax.numpy as jnp
from jax import lax
from jax.experimental import pallas as pl
from jax.experimental.pallas import tpu as pltpu
from jax.sharding import PartitionSpec as P

F32, BF16 = jnp.float32, jnp.bfloat16
LANES = 128
TB = 16
WIDE = 256
KINDS = 3
PARTS = 2
TOGETHER = 2


def iota(shape, axis):
    return lax.broadcasted_iota(jnp.int32, shape, axis)


def flag(condition, kind=BF16):
    return jnp.where(condition, 1.0, 0.0).astype(kind)


def permutation(size):
    return flag(iota((size, size), 0) + iota((size, size), 1) == size - 1)


def chunk_of(shape, kind, chunk):
    return (iota(shape, 1) // chunk).astype(F32).astype(kind)


def swap_chunks(arrays, bits, chunk):
    count = len(arrays)
    turned = [pltpu.roll(a, n * chunk, 1) if n else a for n, a in enumerate(arrays)]
    rows = [turned[(-i) % count] for i in range(count)]
    for power, moved in enumerate(bits):
        bit = 1 << power
        rows = [jnp.where(moved, rows[(i - bit) % count], rows[i]) for i in range(count)]
    return [pltpu.roll(a, LANES - n * chunk, 1) if n else a for n, a in enumerate(rows)]


def chunk_bits(kind, chunk):
    pos = iota((TB, LANES), 1) // chunk
    return [flag((pos >> power) & 1 == 1, kind) > 0 for power in range((LANES // chunk).bit_length() - 1)]


def to_groups(block, bits, chunk):
    per = LANES // chunk
    sets = []
    for first in range(0, block.shape[0], TB * per):
        parts = [block[first + TB * n : first + TB * (n + 1)] for n in range(per)]
        sets.append(swap_chunks(parts, bits, chunk))
    return [[s[g] for s in sets] for g in range(per)]


def from_groups(chunked, bits, chunk):
    rows = []
    for first in range(0, chunked[0].shape[1], LANES):
        rows += swap_chunks([a[:, first : first + LANES] for a in chunked], bits, chunk)
    return jnp.concatenate(rows, axis=0)


def windows(ext, pos, chunk, count):
    per = LANES // chunk
    width = len(ext) - count // per
    out = []
    for i in range(count + 1):
        whole, part = divmod(i, per)
        if part == 0:
            vregs = ext[whole : whole + width]
        else:
            turned = [pltpu.roll(a, LANES - chunk * part, 1) for a in ext[whole : whole + width + 1]]
            vregs = [jnp.where(pos < per - part, turned[v], turned[v + 1]) for v in range(width)]
        out.append(side_by_side(vregs))
    return out


def side_by_side(vregs):
    return vregs[0] if len(vregs) == 1 else jnp.concatenate(vregs, axis=1)


def product_bf16(a, b):
    return (a.astype(F32) * b.astype(F32)).astype(BF16)


def skew_left(products):
    moved = pltpu.roll(products, WIDE - products.shape[0], 1, stride=1, stride_axis=0)
    return jnp.sum(moved, axis=0, keepdims=True)


def shifted_taps(row, first):
    base = jnp.concatenate([row, jnp.zeros((1, WIDE - row.shape[1]), F32)], axis=1)
    base = jnp.broadcast_to(base, (TB, WIDE))
    return pltpu.roll(base, first, 1, stride=1, stride_axis=0).astype(BF16)


def chosen(products, sel_ref):
    return sum(products[kind * TB : (kind + 1) * TB] * sel_ref[kind * TB : (kind + 1) * TB, :] for kind in range(KINDS))


def with_kinds(taps, own, chunk):
    pos = chunk_of((TB, LANES), BF16, chunk)
    zero = jnp.zeros((TB, LANES), BF16)
    further = [jnp.where(pos == kind, pltpu.roll(own, kind * TB, 1), zero) for kind in range(1, KINDS)]
    return jnp.concatenate([taps[:, :LANES], taps[:, LANES:]] + further, axis=0)


def band_of(stored):
    none = jnp.zeros(((KINDS - 1) * TB, LANES), BF16)
    return jnp.concatenate([jnp.concatenate([stored[:TB], none], axis=0), stored[TB:]], axis=1)


def prepare_kernel(chunk, info, q_ref, ct_ref, k_ref, v_ref, taps_ref, x_ref, dy_ref, turned_ref, bx_ref, bdy_ref, gb_ref):
    width = q_ref.shape[1]
    filter_size = taps_ref.shape[1]
    per = LANES // chunk
    for sub in range(width // LANES):
        lanes = pl.ds(sub * LANES, LANES)
        bits = chunk_bits(BF16, chunk)
        x = product_bf16(k_ref[:, lanes], v_ref[:, lanes])
        dy = product_bf16(ct_ref[:, lanes], q_ref[:, lanes])
        gb_ref[:, lanes] = jnp.sum(x.astype(F32) * dy.astype(F32), axis=0, keepdims=True)
        xs, dys = to_groups(x, bits, chunk), to_groups(dy, bits, chunk)
        taps = taps_ref[pl.ds(sub * per, per), :]
        back = jnp.dot(taps.astype(BF16), permutation(filter_size), preferred_element_type=F32)
        for g in range(per):
            at = sub * per + g
            x_ref[at] = side_by_side(xs[g])
            dyg = side_by_side(dys[g])
            dy_ref[at] = dyg
            turned_ref[at] = jnp.dot(permutation(TB), dyg, preferred_element_type=F32).astype(BF16)
            band = shifted_taps(back[g : g + 1], 1)
            bx_ref[at] = with_kinds(band, band[:, LANES:], chunk)
            band = shifted_taps(taps[g : g + 1], 0)
            bdy_ref[at] = with_kinds(band, band[:, :LANES], chunk)


def conv_kernel(chunk, filter_size, info, q_ref, ct_ref, x_ref, turned_ref, taps_ref, bias_ref, rim_ref, mask_ref,
                turned_mask_ref, sel_ref, order_ref, turned_order_ref, *rest):
    out_ref, gq_ref, gf_ref, conv_s, grad_s = rest[-5:]
    width = q_ref.shape[1]
    per = LANES // chunk
    steps = filter_size // TB
    depth = (steps + KINDS) * TB

    def one(sub, slot, further):
        lanes = pl.ds(pl.multiple_of(sub * LANES, LANES), LANES)
        bits, bits32 = chunk_bits(BF16, chunk), chunk_bits(F32, chunk)
        pos = chunk_of((TB, LANES), BF16, chunk)
        kind = KINDS - 1 - iota((KINDS * TB, WIDE), 0) // TB
        col = iota((KINDS * TB, WIDE), 1) - (kind + 1) * TB
        band = (col < filter_size) & ((kind == 0) | (col >= filter_size - TB))
        rims = to_groups(rim_ref[:, lanes], bits, chunk)
        for g in range(per):
            at = sub * per + g
            xg = x_ref[at]
            ext = rims[g] + [xg[:, i : i + LANES] for i in range(0, xg.shape[1], LANES)]
            window = windows(ext, pos, chunk, steps) + [xg] * (KINDS - 1)
            window = jnp.concatenate(window, axis=0) * mask_ref[...]
            y = jnp.dot(band_of(taps_ref[at])[:, :depth], window, preferred_element_type=F32)
            conv_s[slot, g] = chosen(y, sel_ref) + bias_ref[pl.ds(at, 1), :] * xg.astype(F32)
            turned = jnp.concatenate([turned_ref[at]] * KINDS, axis=0) * turned_mask_ref[...]
            pairs = lax.dot_general(turned, window, (((1,), (1,)), ((), ())), preferred_element_type=F32)
            pairs = jnp.concatenate([pairs, jnp.zeros((KINDS * TB, WIDE - depth), F32)], axis=1)
            grad_s[slot, g : g + 1, :] = skew_left(jnp.where(band, pairs, 0.0))

        def more(index, carry):
            level, g = index // per, index % per
            at = sub * per + g
            here = order_ref[...] == level.astype(F32)
            xq = jnp.where(here, x_ref[at].astype(F32), 0.0).astype(BF16)
            turned = turned_order_ref[...] == level.astype(F32)
            turned = jnp.where(turned, turned_ref[at].astype(F32), 0.0).astype(BF16)
            own = taps_ref[at][TB : 2 * TB, :TB]
            conv_s[slot, g] += jnp.where(here, jnp.dot(own, xq, preferred_element_type=F32), 0.0)
            pairs = lax.dot_general(turned, xq, (((1,), (1,)), ((), ())), preferred_element_type=F32)
            pairs = jnp.concatenate(
                [jnp.zeros((TB, filter_size), F32), pairs, jnp.zeros((TB, WIDE - filter_size - TB), F32)], axis=1
            )
            grad_s[slot, pl.ds(g, 1), :] += skew_left(pairs)
            return carry

        if further:
            lax.fori_loop(KINDS * per, info[0] * per, more, 0)
        gf_ref[pl.ds(pl.multiple_of(sub * per, per), per), :] = jnp.dot(
            grad_s[slot, :, :filter_size],
            permutation(filter_size).astype(F32),
            precision=lax.Precision.HIGHEST,
            preferred_element_type=F32,
        )
        filtered = from_groups([conv_s[slot, g] for g in range(per)], bits32, chunk)
        out_ref[:, lanes] = (q_ref[:, lanes].astype(F32) * filtered).astype(BF16)
        gq_ref[:, lanes] = (ct_ref[:, lanes].astype(F32) * filtered).astype(BF16)

    for_all_lanes(one, width // LANES, info)


def back_kernel(chunk, filter_size, info, k_ref, v_ref, dy_ref, taps_ref, bias_ref, rim_ref, mask_ref, sel_ref,
                order_ref, *rest):
    gk_ref, gv_ref, back_s = rest[-3:]
    width = k_ref.shape[1]
    per = LANES // chunk
    steps = filter_size // TB
    depth = (steps + KINDS) * TB

    def one(sub, slot, further):
        lanes = pl.ds(pl.multiple_of(sub * LANES, LANES), LANES)
        bits, bits32 = chunk_bits(BF16, chunk), chunk_bits(F32, chunk)
        pos = chunk_of((TB, LANES), BF16, chunk)
        rims = to_groups(rim_ref[:, lanes], bits, chunk)
        for g in range(per):
            at = sub * per + g
            dyg = dy_ref[at]
            ext = [dyg[:, i : i + LANES] for i in range(0, dyg.shape[1], LANES)] + rims[g]
            window = windows(ext, pos, chunk, steps) + [dyg] * (KINDS - 1)
            window = jnp.concatenate(window, axis=0) * mask_ref[...]
            y = jnp.dot(band_of(taps_ref[at])[:, :depth], window, preferred_element_type=F32)
            back_s[slot, g] = chosen(y, sel_ref) + bias_ref[pl.ds(at, 1), :] * dyg.astype(F32)

        def more(index, carry):
            level, g = index // per, index % per
            at = sub * per + g
            here = order_ref[...] == level.astype(F32)
            dyq = jnp.where(here, dy_ref[at].astype(F32), 0.0).astype(BF16)
            own = taps_ref[at][:TB, :TB]
            back_s[slot, g] += jnp.where(here, jnp.dot(own, dyq, preferred_element_type=F32), 0.0)
            return carry

        if further:
            lax.fori_loop(KINDS * per, info[0] * per, more, 0)
        back = from_groups([back_s[slot, g] for g in range(per)], bits32, chunk)
        gk_ref[:, lanes] = (back * v_ref[:, lanes].astype(F32)).astype(BF16)
        gv_ref[:, lanes] = (back * k_ref[:, lanes].astype(F32)).astype(BF16)

    for_all_lanes(one, width // LANES, info)


def for_all_lanes(one, count, info):
    together = math.gcd(count, TOGETHER)

    def run(further):
        def step(index, carry):
            for slot in range(together):
                one(index * together + slot, slot, further)
            return carry

        lax.fori_loop(0, count // together, step, 0)

    pl.when(info[0] <= KINDS)(lambda: run(False))
    pl.when(info[0] > KINDS)(lambda: run(True))


def call(kernel, name, info, count, ins, outs, scratch=(), previous=None):
    operands = [a for a, _, _ in ins]
    in_specs = [pl.BlockSpec(block, at) for _, block, at in ins]
    aliases = {}
    if previous is not None:
        aliases = {1 + len(operands) + i: i for i in range(len(previous))}
        in_specs += [pl.BlockSpec(memory_space=pl.ANY)] * len(previous)
        operands += list(previous)
    return pl.pallas_call(
        kernel,
        grid_spec=pltpu.PrefetchScalarGridSpec(
            num_scalar_prefetch=1,
            grid=(count,),
            in_specs=in_specs,
            out_specs=[pl.BlockSpec(block, at) for _, _, block, at in outs],
            scratch_shapes=list(scratch),
        ),
        out_shape=[jax.ShapeDtypeStruct(shape, kind) for shape, kind, _, _ in outs],
        input_output_aliases=aliases,
        compiler_params=pltpu.CompilerParams(vmem_limit_bytes=48 * 1024 * 1024),
        cost_estimate=pl.CostEstimate(flops=2**24, bytes_accessed=2**20, transcendentals=0),
        name=name,
    )(info, *operands)


def wide(array, block, first):
    return (array, (array.shape[0], block), lambda i, c: (0, first + i))


def per_group(array, groups, first):
    rest = array.shape[1:]
    return (array, (groups, *rest), lambda i, c: (first + i, *[0] * len(rest)))


def fixed(array):
    return (array, array.shape, lambda i, c: (0, 0))


def prepare(info, big, filters):
    row_count, channels = big[0].shape
    chunk, block = TB, math.gcd(channels, 512)
    groups, total, filter_size = block // chunk, channels // chunk, filters.shape[1]
    taps = (filters, (groups, filter_size), lambda i, c: (c[1] * (channels // block) + i, 0))
    ins = [wide(a, block, 0) for a in big] + [taps]
    shapes = [(TB, row_count)] * 3 + [((1 + KINDS) * TB, LANES)] * 2
    outs = [((total, *s), BF16, (groups, *s), lambda i, c: (i, 0, 0)) for s in shapes]
    outs.append(((1, channels), F32, (1, block), lambda i, c: (0, i)))
    return call(functools.partial(prepare_kernel, chunk), "prepare", info, channels // block, ins, outs)


def run_part(kernel, name, part, info, pair, grouped, rim, rim_first, masks, filter_size, small, previous):
    row_count, channels = pair[0].shape
    chunk, width = TB, channels // PARTS
    block = math.gcd(width, 512)
    groups, first = block // chunk, part * (width // block)
    per = LANES // chunk
    ins = [wide(a, block, first) for a in pair] + [per_group(a, groups, first) for a in grouped]
    ins += [wide(rim, block, rim_first * (width // block))] + [fixed(a) for a in masks]
    outs = [((row_count, channels), BF16, (row_count, block), lambda i, c: (0, first + i))] * 2
    scratch = [pltpu.VMEM((TOGETHER, per, TB, row_count), F32)]
    if small:
        outs += [((channels // chunk, filter_size), F32, (groups, filter_size), lambda i, c: (first + i, 0))]
        scratch += [pltpu.VMEM((TOGETHER, per, WIDE), F32)]
    kernel = functools.partial(kernel, chunk, filter_size)
    return call(kernel, name, info, width // block, ins, outs, scratch, previous)


def reset_kernel(steps, near_ref, mask_x, turned_x, sel_x, order_x, turned_order_x, mask_dy, sel_dy, order_dy, kinds):
    total = near_ref.shape[1]
    rows = total - steps * TB
    near = jnp.clip(near_ref[...], -1024, 1024).astype(F32)
    lane, row = iota((TB, total), 1), iota((TB, total), 0)
    spread = jnp.where(lane % TB == row, jnp.broadcast_to(near, (TB, total)), 0.0)
    same = flag(iota((total, total), 0) // TB == iota((total, total), 1) // TB, F32)
    begin = jnp.dot(spread, same, precision=lax.Precision.HIGHEST, preferred_element_type=F32)
    begin = jnp.floor(begin + 0.5)
    own = begin[:, :rows]
    block = iota((TB, rows), 1) // TB * TB
    pos = (block + iota((TB, rows), 0)).astype(F32)
    marks = flag((own == pos) & (iota((TB, rows), 0) > 0))
    before = flag(iota((TB, TB), 0) >= iota((TB, TB), 1))
    order = jnp.dot(before, marks, preferred_element_type=F32)
    behind = order[TB - 1 :] - order
    first = jnp.broadcast_to(own[:1], (TB, rows))
    for i in range(steps):
        mask_x[i * TB : (i + 1) * TB, :] = flag(pos - TB * (steps - i) >= first)
        later = pltpu.roll(begin, total - (i + 1) * TB, 1)[:, :rows]
        mask_dy[(i + 1) * TB : (i + 2) * TB, :] = flag(later <= (block + TB - 1).astype(F32))
    turn = permutation(TB)
    for kind in range(KINDS):
        at = steps + kind
        mask_x[at * TB : (at + 1) * TB, :] = flag(order == kind)
        sel_x[kind * TB : (kind + 1) * TB, :] = flag(order == kind, F32)
        at = KINDS - 1 - kind
        turned = jnp.dot(turn, flag(order == kind), preferred_element_type=F32)
        turned_x[at * TB : (at + 1) * TB, :] = turned.astype(BF16)
        at = steps + kind if kind else 0
        mask_dy[at * TB : (at + 1) * TB, :] = flag(behind == kind)
        sel_dy[kind * TB : (kind + 1) * TB, :] = flag(behind == kind, F32)
    order_x[...], order_dy[...] = order, behind
    turned_order_x[...] = jnp.dot(turn, order.astype(BF16), preferred_element_type=F32)
    kinds[0] = 1 + jnp.max(order).astype(jnp.int32)


def reset_masks(near, row_count, steps):
    depth, high = (steps + KINDS) * TB, KINDS * TB
    shapes = [(depth, BF16), (high, BF16), (high, F32), (TB, F32), (TB, F32), (depth, BF16), (high, F32), (TB, F32)]
    out = pl.pallas_call(
        functools.partial(reset_kernel, steps),
        out_shape=[jax.ShapeDtypeStruct((rows, row_count), kind) for rows, kind in shapes]
        + [jax.ShapeDtypeStruct((1,), jnp.int32)],
        out_specs=[pl.BlockSpec(memory_space=pltpu.VMEM)] * len(shapes) + [pl.BlockSpec(memory_space=pltpu.SMEM)],
        compiler_params=pltpu.CompilerParams(vmem_limit_bytes=32 * 1024 * 1024),
        name="resets",
    )(near)
    return out[:5], out[5:8], out[8]


def passed_along(value, axis, steps):
    count = lax.axis_size(axis)
    initial, last = (max(0, -steps), min(count, count - steps))
    return lax.ppermute(value, axis, [(source, source + steps) for source in range(initial, last)])


def sum_over(value, axis):
    count = lax.axis_size(axis)
    if count & (count - 1):
        return lax.psum(value, axis)
    step = 1
    while step < count:
        value = value + lax.ppermute(value, axis, [(i, i ^ step) for i in range(count)])
        step *= 2
    return value


def rows_of_all(value, axis):
    count = lax.axis_size(axis)
    if count != 2:
        return lax.all_gather(value, axis, axis=0, tiled=True)
    other = lax.ppermute(value, axis, [(0, 1), (1, 0)])
    is_first = lax.axis_index(axis) == 0
    return jnp.concatenate([jnp.where(is_first, value, other), jnp.where(is_first, other, value)], axis=0)


def body(queries, key_branch, value_branch, cotangent, filters, skip_bias, contig_start):
    row_count, channels = queries.shape
    group_total, filter_size = filters.shape
    ctx_count, tp_count = lax.axis_size("ctx"), lax.axis_size("tp")
    shard, tensor = lax.axis_index("ctx"), lax.axis_index("tp")
    token_count = row_count * ctx_count
    chunk = channels * tp_count // group_total
    groups = channels // chunk
    width = channels // PARTS

    tail = lambda m: m[row_count - filter_size :]
    left = passed_along(product_bf16(tail(key_branch), tail(value_branch)), "ctx", 1)

    starts = jnp.concatenate([contig_start, jnp.full((filter_size,), 2**30, jnp.int32)])
    first = shard * row_count
    near = (lax.dynamic_slice_in_dim(starts, first, row_count + filter_size, 0) - first)[None, :]
    masks_x, masks_dy, kinds = reset_masks(near, row_count, filter_size // TB)
    info = jnp.concatenate([kinds, tensor.astype(jnp.int32).reshape(1)])
    bias = jnp.tile(skip_bias.reshape(groups, chunk), (1, row_count // TB))
    big = (queries, cotangent, key_branch, value_branch)
    x, dy, turned, band_x, band_dy, bias_part = prepare(info, big, filters)

    right = []
    for part in range(PARTS):
        cut = lambda m: lax.slice(m, (0, part * width), (filter_size, (part + 1) * width))
        sent = product_bf16(cut(cotangent), cut(queries))
        if part:
            sent, right[-1] = lax.optimization_barrier((sent, right[-1]))
        else:
            sent, bias_part = lax.optimization_barrier((sent, bias_part))
        right.append(passed_along(sent, "ctx", -1))

    done, rim = None, left
    for part in range(PARTS):
        grouped = (x, turned, band_x, bias)
        done = run_part(
            conv_kernel, "conv", part, info, (queries, cotangent), grouped, rim, part, masks_x, filter_size, True, done
        )
    output, grad_query, filter_part = done
    done = None
    for part in range(PARTS):
        grouped = (dy, band_dy, bias)
        pair = (key_branch, value_branch)
        done = run_part(
            back_kernel, "back", part, info, pair, grouped, right[part], 0, masks_dy, filter_size, False, done
        )
    grad_key, grad_value = done

    terms = jnp.concatenate([filter_part, bias_part.reshape(channels // filter_size, filter_size)], axis=0)
    terms = sum_over(terms, "ctx")
    grad_filter = rows_of_all(terms[:groups], "tp") * (1.0 / math.sqrt(token_count * chunk))
    grad_bias = terms[groups:].reshape(channels) * (1.0 / math.sqrt(token_count))
    return (output, grad_query, grad_key, grad_value, grad_filter, grad_bias)


def solution(mesh):
    whole = P("ctx", "tp")
    return jax.shard_map(
        body,
        mesh=mesh,
        in_specs=(whole, whole, whole, whole, P(), P("tp"), P()),
        out_specs=(whole, whole, whole, whole, P(), P("tp")),
        check_vma=False,
    )
```

```python
import functools
import math

import jax
import jax.numpy as jnp
from jax import lax
from jax.experimental import pallas as pl
from jax.experimental.pallas import tpu as pltpu
from jax.sharding import PartitionSpec as P

F32, BF16 = jnp.float32, jnp.bfloat16
LANES = 128
TB = 16
WIDE = 256
KINDS = 3
PARTS = 2
VMEM_BYTES = 60 * 1024 * 1024
TOGETHER = 2


def iota(shape, axis):
    return lax.broadcasted_iota(jnp.int32, shape, axis)


def flag(condition, kind=BF16):
    return jnp.where(condition, 1.0, 0.0).astype(kind)


def permutation(size):
    return flag(iota((size, size), 0) + iota((size, size), 1) == size - 1)


def chunk_of(shape, kind, chunk):
    return (iota(shape, 1) // chunk).astype(F32).astype(kind)


def swap_chunks(arrays, bits):
    count = len(arrays)
    rows = [arrays[(-i) % count] for i in range(count)]
    for power, moved in enumerate(bits):
        bit = 1 << power
        rows = [jnp.where(moved, rows[(i - bit) % count], rows[i]) for i in range(count)]
    return rows


def chunk_bits(kind, chunk):
    pos = iota((TB, LANES), 1) // chunk
    return [flag((pos >> power) & 1 == 1, kind) > 0 for power in range((LANES // chunk).bit_length() - 1)]


def to_groups(block, bits, chunk):
    per = LANES // chunk
    sets = []
    for first in range(0, block.shape[0], TB * per):
        parts = [block[first + TB * n : first + TB * (n + 1)] for n in range(per)]
        sets.append(swap_chunks([pltpu.roll(a, n * chunk, 1) if n else a for n, a in enumerate(parts)], bits))
    return [[s[g] for s in sets] for g in range(per)]


def from_groups(chunked, bits, chunk):
    rows = []
    for first in range(0, chunked[0].shape[1], LANES):
        parts = swap_chunks([a[:, first : first + LANES] for a in chunked], bits)
        rows += [pltpu.roll(a, LANES - n * chunk, 1) if n else a for n, a in enumerate(parts)]
    return jnp.concatenate(rows, axis=0)


def place_of(g, chunk):
    per = LANES // chunk
    return ((iota((TB, LANES), 1) // chunk + per - g) % per).astype(F32).astype(BF16)


def past_windows(ext, place, chunk, count):
    per = LANES // chunk
    out = []
    for back in range(count, -1, -1):
        whole, part = divmod(back, per)
        width = len(ext) - count // per
        vregs = []
        for v in range(width):
            near = len(ext) - width + v - whole
            if part:
                vregs.append(pltpu.roll(jnp.where(place < per - part, ext[near], ext[near - 1]), part * chunk, 1))
            else:
                vregs.append(ext[near])
        out.append(side_by_side(vregs))
    return out


def next_windows(ext, place, chunk, count):
    per = LANES // chunk
    width = len(ext) - count // per
    out = []
    for ahead in range(count + 1):
        whole, part = divmod(ahead, per)
        vregs = []
        for v in range(width):
            near = v + whole
            if part:
                vregs.append(pltpu.roll(jnp.where(place >= part, ext[near], ext[near + 1]), LANES - part * chunk, 1))
            else:
                vregs.append(ext[near])
        out.append(side_by_side(vregs))
    return out


def side_by_side(vregs):
    return vregs[0] if len(vregs) == 1 else jnp.concatenate(vregs, axis=1)


def product_bf16(a, b):
    return (a.astype(F32) * b.astype(F32)).astype(BF16)


def skew_left(products):
    moved = pltpu.roll(products, LANES - TB, 1, stride=1, stride_axis=0)
    return moved[: TB // 2] + moved[TB // 2 :]


def exact_dot(a, b):
    return jnp.dot(a, b, precision=lax.Precision.HIGHEST, preferred_element_type=F32)


def group_rows(count, size):
    return flag(iota((count, count * size), 1) // size == iota((count, count * size), 0), F32)


def shifted_taps(row, first):
    base = jnp.concatenate([row, jnp.zeros((1, WIDE - row.shape[1]), F32)], axis=1)
    base = jnp.broadcast_to(base, (TB, WIDE))
    return pltpu.roll(base, first, 1, stride=1, stride_axis=0).astype(BF16)


def chosen(products, sel_ref, g):
    return sum(
        products[kind * TB : (kind + 1) * TB] * sel_ref[g, kind * TB : (kind + 1) * TB, :] for kind in range(KINDS)
    )


def with_kinds(taps, own, chunk):
    pos = chunk_of((TB, LANES), BF16, chunk)
    zero = jnp.zeros((TB, LANES), BF16)
    further = [jnp.where(pos == kind, pltpu.roll(own, kind * TB, 1), zero) for kind in range(1, KINDS)]
    return jnp.concatenate([taps[:, :LANES], taps[:, LANES:]] + further, axis=0)


def band_of(stored):
    none = jnp.zeros(((KINDS - 1) * TB, LANES), BF16)
    return jnp.concatenate([jnp.concatenate([stored[:TB], none], axis=0), stored[TB:]], axis=1)


def prepare_kernel(chunk, info, q_ref, ct_ref, k_ref, v_ref, taps_ref, x_ref, dy_ref, turned_ref, bx_ref, bdy_ref, gb_ref, head_ref):
    width = q_ref.shape[1]
    filter_size = taps_ref.shape[1]
    per = LANES // chunk
    for sub in range(width // LANES):
        lanes = pl.ds(sub * LANES, LANES)
        bits = chunk_bits(BF16, chunk)
        x = product_bf16(k_ref[:, lanes], v_ref[:, lanes])
        dy = product_bf16(ct_ref[:, lanes], q_ref[:, lanes])
        gb_ref[:, lanes] = jnp.sum(x.astype(F32) * dy.astype(F32), axis=0, keepdims=True)
        head_ref[:, lanes] = dy[:filter_size]
        xs, dys = to_groups(x, bits, chunk), to_groups(dy, bits, chunk)
        taps = taps_ref[pl.ds(sub * per, per), :]
        back = jnp.dot(taps.astype(BF16), permutation(filter_size), preferred_element_type=F32)
        for g in range(per):
            at = sub * per + g
            x_ref[at] = side_by_side(xs[g])
            dyg = side_by_side(dys[g])
            dy_ref[at] = dyg
            turned_ref[at] = jnp.dot(permutation(TB), dyg, preferred_element_type=F32).astype(BF16)
            band = shifted_taps(back[g : g + 1], 1)
            bx_ref[at] = with_kinds(band, band[:, LANES:], chunk)
            band = shifted_taps(taps[g : g + 1], 0)
            bdy_ref[at] = with_kinds(band, band[:, :LANES], chunk)


def conv_kernel(chunk, filter_size, info, q_ref, ct_ref, x_ref, turned_ref, taps_ref, bias_ref, rim_ref, mask_ref,
                turned_mask_ref, sel_ref, order_ref, turned_order_ref, *rest):
    out_ref, gq_ref, gf_ref, conv_s, grad_s = rest[-5:]
    width = q_ref.shape[1]
    per = LANES // chunk
    steps = filter_size // TB
    depth = (steps + KINDS) * TB

    def one(sub, slot, further):
        lanes = pl.ds(pl.multiple_of(sub * LANES, LANES), LANES)
        bits, bits32 = chunk_bits(BF16, chunk), chunk_bits(F32, chunk)
        late, lane = TB - 1 - iota((TB, LANES), 0), iota((TB, LANES), 1)
        causal = lane % TB <= late
        rims = to_groups(rim_ref[:, lanes], bits, chunk)
        for g in range(per):
            at = sub * per + g
            xg = x_ref[at]
            ext = rims[g] + [xg[:, i : i + LANES] for i in range(0, xg.shape[1], LANES)]
            window = past_windows(ext, place_of(g, chunk), chunk, steps) + [xg] * (KINDS - 1)
            window = jnp.concatenate(window, axis=0) * mask_ref[g]
            y = jnp.dot(band_of(taps_ref[at])[:, :depth], window, preferred_element_type=F32)
            conv_s[slot, g] = chosen(y, sel_ref, g) + bias_ref[pl.ds(at, 1), :] * xg.astype(F32)
            turned = jnp.concatenate([turned_ref[at]] * KINDS, axis=0) * turned_mask_ref[g]
            pairs = lax.dot_general(turned, window, (((1,), (1,)), ((), ())), preferred_element_type=F32)
            pairs = jnp.concatenate([pairs, jnp.zeros((KINDS * TB, WIDE - depth), F32)], axis=1)
            half = TB // 2
            far = pairs[(KINDS - 1) * TB :, :LANES]
            grad_s[slot, 0, g * half : (g + 1) * half, :] = skew_left(jnp.where(lane > late, far, 0.0))
            own = jnp.zeros((TB, LANES), F32)
            for kind in range(KINDS):
                first = (KINDS - 1 - kind) * TB
                own = jnp.where(causal & (lane // TB == kind), pairs[first : first + TB, LANES:], own)
            grad_s[slot, 1, g * half : (g + 1) * half, :] = skew_left(own)

        def more(index, carry):
            level, g = index // per, index % per
            at = sub * per + g
            here = order_ref[g] == level.astype(F32)
            xq = jnp.where(here, x_ref[at].astype(F32), 0.0).astype(BF16)
            turned = turned_order_ref[g] == level.astype(F32)
            turned = jnp.where(turned, turned_ref[at].astype(F32), 0.0).astype(BF16)
            own = taps_ref[at][TB : 2 * TB, :TB]
            conv_s[slot, g] += jnp.where(here, jnp.dot(own, xq, preferred_element_type=F32), 0.0)
            pairs = lax.dot_general(turned, xq, (((1,), (1,)), ((), ())), preferred_element_type=F32)
            pairs = jnp.concatenate([pairs, jnp.zeros((TB, LANES - TB), F32)], axis=1)
            rows = pl.ds(pl.multiple_of(g * (TB // 2), TB // 2), TB // 2)
            grad_s[slot, 1, rows, :] += skew_left(jnp.where(causal & (lane < TB), pairs, 0.0))
            return carry

        if further:
            lax.fori_loop(KINDS * per, info[0] * per, more, 0)
        own = exact_dot(group_rows(per, TB // 2), grad_s[slot, 1])
        terms = exact_dot(group_rows(per, TB // 2), grad_s[slot, 0])
        last = iota((per, LANES), 1) >= LANES - TB
        for kind in range(KINDS):
            shift = (LANES - kind * TB) % LANES
            terms += jnp.where(last, pltpu.roll(own, shift, 1) if shift else own, 0.0)
        gf_ref[pl.ds(pl.multiple_of(sub * per, per), per), :] = exact_dot(terms, permutation(LANES).astype(F32))
        filtered = from_groups([conv_s[slot, g] for g in range(per)], bits32, chunk)
        out_ref[:, lanes] = (q_ref[:, lanes].astype(F32) * filtered).astype(BF16)
        gq_ref[:, lanes] = (ct_ref[:, lanes].astype(F32) * filtered).astype(BF16)

    for_all_lanes(one, width // LANES, info)


def back_kernel(chunk, filter_size, info, k_ref, v_ref, dy_ref, taps_ref, bias_ref, rim_ref, mask_ref, sel_ref,
                order_ref, *rest):
    gk_ref, gv_ref, token_ref, back_s = rest[-4:]
    token_ref[...] = jnp.zeros_like(token_ref)
    width = k_ref.shape[1]
    per = LANES // chunk
    steps = filter_size // TB
    depth = (steps + KINDS) * TB

    def one(sub, slot, further):
        lanes = pl.ds(pl.multiple_of(sub * LANES, LANES), LANES)
        bits, bits32 = chunk_bits(BF16, chunk), chunk_bits(F32, chunk)
        rims = to_groups(rim_ref[:, lanes], bits, chunk)
        for g in range(per):
            at = sub * per + g
            dyg = dy_ref[at]
            ext = [dyg[:, i : i + LANES] for i in range(0, dyg.shape[1], LANES)] + rims[g]
            window = next_windows(ext, place_of(g, chunk), chunk, steps) + [dyg] * (KINDS - 1)
            window = jnp.concatenate(window, axis=0) * mask_ref[g]
            y = jnp.dot(band_of(taps_ref[at])[:, :depth], window, preferred_element_type=F32)
            back_s[slot, g] = chosen(y, sel_ref, g) + bias_ref[pl.ds(at, 1), :] * dyg.astype(F32)

        def more(index, carry):
            level, g = index // per, index % per
            at = sub * per + g
            here = order_ref[g] == level.astype(F32)
            dyq = jnp.where(here, dy_ref[at].astype(F32), 0.0).astype(BF16)
            own = taps_ref[at][:TB, :TB]
            back_s[slot, g] += jnp.where(here, jnp.dot(own, dyq, preferred_element_type=F32), 0.0)
            return carry

        if further:
            lax.fori_loop(KINDS * per, info[0] * per, more, 0)
        back = from_groups([back_s[slot, g] for g in range(per)], bits32, chunk)
        gk_ref[:, lanes] = (back * v_ref[:, lanes].astype(F32)).astype(BF16)
        gv_ref[:, lanes] = (back * k_ref[:, lanes].astype(F32)).astype(BF16)

    for_all_lanes(one, width // LANES, info)


def for_all_lanes(one, count, info):
    together = math.gcd(count, TOGETHER)

    def run(further):
        def step(index, carry):
            for slot in range(together):
                one(index * together + slot, slot, further)
            return carry

        lax.fori_loop(0, count // together, step, 0)

    pl.when(info[0] <= KINDS)(lambda: run(False))
    pl.when(info[0] > KINDS)(lambda: run(True))


def call(kernel, name, info, count, ins, outs, scratch=(), previous=None):
    operands = [a for a, _, _ in ins]
    in_specs = [pl.BlockSpec(block, at) for _, block, at in ins]
    aliases = {}
    if previous is not None:
        aliases = {1 + len(operands) + i: i for i in range(len(previous))}
        in_specs += [pl.BlockSpec(memory_space=pl.ANY)] * len(previous)
        operands += list(previous)
    return pl.pallas_call(
        kernel,
        grid_spec=pltpu.PrefetchScalarGridSpec(
            num_scalar_prefetch=1,
            grid=(count,),
            in_specs=in_specs,
            out_specs=[pl.BlockSpec(block, at) for _, _, block, at in outs],
            scratch_shapes=list(scratch),
        ),
        out_shape=[jax.ShapeDtypeStruct(shape, kind) for shape, kind, _, _ in outs],
        input_output_aliases=aliases,
        compiler_params=pltpu.CompilerParams(vmem_limit_bytes=VMEM_BYTES),
        cost_estimate=pl.CostEstimate(flops=2**24, bytes_accessed=2**20, transcendentals=0),
        name=name,
    )(info, *operands)


def wide(array, block, first):
    return (array, (array.shape[0], block), lambda i, c: (0, first + i))


def per_group(array, groups, first):
    rest = array.shape[1:]
    return (array, (groups, *rest), lambda i, c: (first + i, *[0] * len(rest)))


def fixed(array):
    return (array, array.shape, lambda i, c: (0, 0, 0))


def prepare(info, big, filters):
    row_count, channels = big[0].shape
    chunk, block = TB, math.gcd(channels, 512)
    groups, total, filter_size = block // chunk, channels // chunk, filters.shape[1]
    taps = (filters, (groups, filter_size), lambda i, c: (c[1] * (channels // block) + i, 0))
    ins = [wide(a, block, 0) for a in big] + [taps]
    shapes = [(TB, row_count)] * 3 + [((1 + KINDS) * TB, LANES)] * 2
    outs = [((total, *s), BF16, (groups, *s), lambda i, c: (i, 0, 0)) for s in shapes]
    outs.append(((1, channels), F32, (1, block), lambda i, c: (0, i)))
    outs.append(((filter_size, channels), BF16, (filter_size, block), lambda i, c: (0, i)))
    return call(functools.partial(prepare_kernel, chunk), "prepare", info, channels // block, ins, outs)


def run_part(kernel, name, part, info, pair, grouped, rim, rim_first, masks, filter_size, small, previous):
    row_count, channels = pair[0].shape
    chunk, width = TB, channels // PARTS
    block = math.gcd(width, 512)
    groups, first = block // chunk, part * (width // block)
    per = LANES // chunk
    ins = [wide(a, block, first) for a in pair] + [per_group(a, groups, first) for a in grouped]
    ins += [wide(rim, block, rim_first * (width // block))] + [fixed(a) for a in masks]
    outs = [((row_count, channels), BF16, (row_count, block), lambda i, c: (0, first + i))] * 2
    scratch = [pltpu.VMEM((TOGETHER, per, TB, row_count), F32)]
    if small:
        outs += [((channels // chunk, filter_size), F32, (groups, filter_size), lambda i, c: (first + i, 0))]
        scratch += [pltpu.VMEM((TOGETHER, 2, per * TB // 2, LANES), F32)]
    else:
        outs += [((8, LANES), F32, (8, LANES), lambda i, c: (0, 0))]
    kernel = functools.partial(kernel, chunk, filter_size)
    return call(kernel, name, info, width // block, ins, outs, scratch, previous)


def reset_kernel(steps, near_ref, mask_x, turned_x, sel_x, order_x, turned_order_x, mask_dy, sel_dy, order_dy, kinds):
    total = near_ref.shape[1]
    rows = total - steps * TB
    near = jnp.clip(near_ref[...], -1024, 1024).astype(F32)
    lane, row = iota((TB, total), 1), iota((TB, total), 0)
    spread = jnp.where(lane % TB == row, jnp.broadcast_to(near, (TB, total)), 0.0)
    same = flag(iota((total, total), 0) // TB == iota((total, total), 1) // TB, F32)
    begin = jnp.floor(exact_dot(spread, same) + 0.5)
    own = begin[:, :rows]
    block = iota((TB, rows), 1) // TB * TB
    pos = (block + iota((TB, rows), 0)).astype(F32)
    marks = flag((own == pos) & (iota((TB, rows), 0) > 0))
    before = flag(iota((TB, TB), 0) >= iota((TB, TB), 1))
    order = jnp.dot(before, marks, preferred_element_type=F32)
    behind = order[TB - 1 :] - order
    first = jnp.broadcast_to(own[:1], (TB, rows))
    turn = permutation(TB)

    def put(ref, at, value):
        parts = [value[:, i : i + LANES] for i in range(0, rows, LANES)]
        for g in range(ref.shape[0]):
            turned = side_by_side([pltpu.roll(a, g * TB, 1) if g else a for a in parts])
            ref[g, at * TB : (at + 1) * TB, :] = turned.astype(ref.dtype)

    for i in range(steps):
        put(mask_x, i, flag(pos - TB * (steps - i) >= first, F32))
        later = pltpu.roll(begin, total - (i + 1) * TB, 1)[:, :rows]
        put(mask_dy, i + 1, flag(later <= (block + TB - 1).astype(F32), F32))
    for kind in range(KINDS):
        put(mask_x, steps + kind, flag(order == kind, F32))
        put(sel_x, kind, flag(order == kind, F32))
        put(turned_x, KINDS - 1 - kind, jnp.dot(turn, flag(order == kind), preferred_element_type=F32))
        put(mask_dy, steps + kind if kind else 0, flag(behind == kind, F32))
        put(sel_dy, kind, flag(behind == kind, F32))
    put(order_x, 0, order)
    put(order_dy, 0, behind)
    put(turned_order_x, 0, jnp.dot(turn, order.astype(BF16), preferred_element_type=F32))
    kinds[0] = 1 + jnp.max(order).astype(jnp.int32)


def reset_masks(near, row_count, steps):
    depth, high, per = (steps + KINDS) * TB, KINDS * TB, LANES // TB
    shapes = [(depth, BF16), (high, BF16), (high, F32), (TB, F32), (TB, F32), (depth, BF16), (high, F32), (TB, F32)]
    out = pl.pallas_call(
        functools.partial(reset_kernel, steps),
        out_shape=[jax.ShapeDtypeStruct((per, rows, row_count), kind) for rows, kind in shapes]
        + [jax.ShapeDtypeStruct((1,), jnp.int32)],
        out_specs=[pl.BlockSpec(memory_space=pltpu.VMEM)] * len(shapes) + [pl.BlockSpec(memory_space=pltpu.SMEM)],
        compiler_params=pltpu.CompilerParams(vmem_limit_bytes=VMEM_BYTES),
        name="resets",
    )(near)
    return out[:5], out[5:8], out[8]


def passed_along(value, axis, steps):
    count = lax.axis_size(axis)
    initial, last = (max(0, -steps), min(count, count - steps))
    return lax.ppermute(value, axis, [(source, source + steps) for source in range(initial, last)])


def sum_over(value, axis, tokens):
    count = lax.axis_size(axis)
    if count & (count - 1):
        return lax.psum(value, axis)
    steps = count.bit_length() - 1
    for index in range(steps):
        other = lax.ppermute(value, axis, [(i, i ^ (1 << index)) for i in range(count)])
        if index % 2 == 0 and index // 2 < len(tokens):
            other = other + tokens[index // 2][0, 0]
        value = value + other
    return value


def rows_of_all(value, axis):
    count = lax.axis_size(axis)
    if count != 2:
        return lax.all_gather(value, axis, axis=0, tiled=True)
    other = lax.ppermute(value, axis, [(0, 1), (1, 0)])
    is_first = lax.axis_index(axis) == 0
    return jnp.concatenate([jnp.where(is_first, value, other), jnp.where(is_first, other, value)], axis=0)


def body(queries, key_branch, value_branch, cotangent, filters, skip_bias, contig_start):
    row_count, channels = queries.shape
    group_total, filter_size = filters.shape
    ctx_count, tp_count = lax.axis_size("ctx"), lax.axis_size("tp")
    shard, tensor = lax.axis_index("ctx"), lax.axis_index("tp")
    token_count = row_count * ctx_count
    chunk = channels * tp_count // group_total
    groups = channels // chunk
    width = channels // PARTS

    tail = lambda m: m[row_count - filter_size :]
    left = passed_along(product_bf16(tail(key_branch), tail(value_branch)), "ctx", 1)

    starts = jnp.concatenate([contig_start, jnp.full((filter_size,), 2**30, jnp.int32)])
    first = shard * row_count
    near = (lax.dynamic_slice_in_dim(starts, first, row_count + filter_size, 0) - first)[None, :]
    masks_x, masks_dy, kinds = reset_masks(near, row_count, filter_size // TB)
    info = jnp.concatenate([kinds, tensor.astype(jnp.int32).reshape(1)])
    bias = jnp.tile(skip_bias.reshape(groups, chunk), (1, row_count // TB))
    big = (queries, cotangent, key_branch, value_branch)
    place = jnp.stack([tensor, tensor]).astype(jnp.int32)
    x, dy, turned, band_x, band_dy, bias_part, head = prepare(place, big, filters)

    right = passed_along(head, "ctx", -1)

    done = None
    for part in range(PARTS):
        grouped = (x, turned, band_x, bias)
        pair = (queries, cotangent)
        done = run_part(conv_kernel, "conv", part, info, pair, grouped, left, part, masks_x, filter_size, True, done)
    output, grad_query, filter_part = done
    terms = jnp.concatenate([filter_part, bias_part.reshape(channels // filter_size, filter_size)], axis=0)

    done, tokens = None, []
    for part in range(PARTS):
        grouped = (dy, band_dy, bias)
        pair = (key_branch, value_branch)
        *done, token = run_part(
            back_kernel, "back", part, info, pair, grouped, right, part, masks_dy, filter_size, False, done
        )
        tokens.append(token)
    grad_key, grad_value = done

    terms = sum_over(terms, "ctx", tokens)
    grad_filter = rows_of_all(terms[:groups], "tp") * (1.0 / math.sqrt(token_count * chunk))
    grad_bias = terms[groups:].reshape(channels) * (1.0 / math.sqrt(token_count))
    return (output, grad_query, grad_key, grad_value, grad_filter, grad_bias)


def solution(mesh):
    whole = P("ctx", "tp")
    return jax.shard_map(
        body,
        mesh=mesh,
        in_specs=(whole, whole, whole, whole, P(), P("tp"), P()),
        out_specs=(whole, whole, whole, whole, P(), P("tp")),
        check_vma=False,
    )
```

```python
import functools
import math

import jax
import jax.numpy as jnp
from jax import lax
from jax.experimental import pallas as pl
from jax.experimental.pallas import tpu as pltpu
from jax.sharding import PartitionSpec as P

F32, BF16 = jnp.float32, jnp.bfloat16
LANES = 128
TB = 16
WIDE = 256
KINDS = 3
BACK_PARTS = 4
VMEM_BYTES = 60 * 1024 * 1024
TOGETHER = 2


def iota(shape, axis):
    return lax.broadcasted_iota(jnp.int32, shape, axis)


def flag(condition, kind=BF16):
    return jnp.where(condition, 1.0, 0.0).astype(kind)


def permutation(size):
    return flag(iota((size, size), 0) + iota((size, size), 1) == size - 1)


def chunk_of(shape, kind, chunk):
    return (iota(shape, 1) // chunk).astype(F32).astype(kind)


def swap_chunks(arrays, bits):
    count = len(arrays)
    rows = [arrays[(-i) % count] for i in range(count)]
    for power, moved in enumerate(bits):
        bit = 1 << power
        rows = [jnp.where(moved, rows[(i - bit) % count], rows[i]) for i in range(count)]
    return rows


def chunk_bits(kind, chunk):
    pos = iota((TB, LANES), 1) // chunk
    return [flag((pos >> power) & 1 == 1, kind) > 0 for power in range((LANES // chunk).bit_length() - 1)]


def to_groups(block, bits, chunk):
    per = LANES // chunk
    sets = []
    for first in range(0, block.shape[0], TB * per):
        parts = [block[first + TB * n : first + TB * (n + 1)] for n in range(per)]
        sets.append(swap_chunks([pltpu.roll(a, n * chunk, 1) if n else a for n, a in enumerate(parts)], bits))
    return [[s[g] for s in sets] for g in range(per)]


def from_groups(chunked, bits, chunk):
    rows = []
    for first in range(0, chunked[0].shape[1], LANES):
        parts = swap_chunks([a[:, first : first + LANES] for a in chunked], bits)
        rows += [pltpu.roll(a, LANES - n * chunk, 1) if n else a for n, a in enumerate(parts)]
    return jnp.concatenate(rows, axis=0)


def place_of(g, chunk):
    per = LANES // chunk
    return ((iota((TB, LANES), 1) // chunk + per - g) % per).astype(F32).astype(BF16)


def past_windows(ext, place, chunk, count):
    per = LANES // chunk
    out = []
    for back in range(count, -1, -1):
        whole, part = divmod(back, per)
        width = len(ext) - count // per
        vregs = []
        for v in range(width):
            near = len(ext) - width + v - whole
            if part:
                vregs.append(pltpu.roll(jnp.where(place < per - part, ext[near], ext[near - 1]), part * chunk, 1))
            else:
                vregs.append(ext[near])
        out.append(side_by_side(vregs))
    return out


def next_windows(ext, place, chunk, count):
    per = LANES // chunk
    width = len(ext) - count // per
    out = []
    for ahead in range(count + 1):
        whole, part = divmod(ahead, per)
        vregs = []
        for v in range(width):
            near = v + whole
            if part:
                vregs.append(pltpu.roll(jnp.where(place >= part, ext[near], ext[near + 1]), LANES - part * chunk, 1))
            else:
                vregs.append(ext[near])
        out.append(side_by_side(vregs))
    return out


def side_by_side(vregs):
    return vregs[0] if len(vregs) == 1 else jnp.concatenate(vregs, axis=1)


def product_bf16(a, b):
    return (a.astype(F32) * b.astype(F32)).astype(BF16)


def skew_left(products):
    moved = pltpu.roll(products, LANES - TB, 1, stride=1, stride_axis=0)
    return jnp.sum(moved, axis=0, keepdims=True)


def exact_dot(a, b):
    return jnp.dot(a, b, precision=lax.Precision.HIGHEST, preferred_element_type=F32)


def shifted_taps(row, first):
    base = jnp.concatenate([row, jnp.zeros((1, WIDE - row.shape[1]), F32)], axis=1)
    base = jnp.broadcast_to(base, (TB, WIDE))
    return pltpu.roll(base, first, 1, stride=1, stride_axis=0).astype(BF16)


def chosen(products, sel_ref, g):
    return sum(
        products[kind * TB : (kind + 1) * TB] * sel_ref[g, kind * TB : (kind + 1) * TB, :] for kind in range(KINDS)
    )


def with_kinds(taps, own, chunk):
    pos = chunk_of((TB, LANES), BF16, chunk)
    zero = jnp.zeros((TB, LANES), BF16)
    further = [jnp.where(pos == kind, pltpu.roll(own, kind * TB, 1), zero) for kind in range(1, KINDS)]
    return jnp.concatenate([taps[:, :LANES], taps[:, LANES:]] + further, axis=0)


def band_of(stored):
    none = jnp.zeros(((KINDS - 1) * TB, LANES), BF16)
    return jnp.concatenate([jnp.concatenate([stored[:TB], none], axis=0), stored[TB:]], axis=1)


def prepare_kernel(chunk, info, q_ref, ct_ref, k_ref, v_ref, taps_ref, x_ref, dy_ref, turned_ref, bx_ref, bdy_ref, gb_ref, head_ref):
    width = q_ref.shape[1]
    filter_size = taps_ref.shape[1]
    per = LANES // chunk
    for sub in range(width // LANES):
        lanes = pl.ds(sub * LANES, LANES)
        bits = chunk_bits(BF16, chunk)
        x = product_bf16(k_ref[:, lanes], v_ref[:, lanes])
        dy = product_bf16(ct_ref[:, lanes], q_ref[:, lanes])
        gb_ref[:, lanes] = jnp.sum(x.astype(F32) * dy.astype(F32), axis=0, keepdims=True)
        head_ref[:, lanes] = dy[:filter_size]
        xs, dys = to_groups(x, bits, chunk), to_groups(dy, bits, chunk)
        taps = taps_ref[pl.ds(sub * per, per), :]
        back = jnp.dot(taps.astype(BF16), permutation(filter_size), preferred_element_type=F32)
        for g in range(per):
            at = sub * per + g
            x_ref[at] = side_by_side(xs[g])
            dyg = side_by_side(dys[g])
            dy_ref[at] = dyg
            turned_ref[at] = jnp.dot(permutation(TB), dyg, preferred_element_type=F32).astype(BF16)
            band = shifted_taps(back[g : g + 1], 1)
            bx_ref[at] = with_kinds(band, band[:, LANES:], chunk)
            band = shifted_taps(taps[g : g + 1], 0)
            bdy_ref[at] = with_kinds(band, band[:, :LANES], chunk)


def conv_kernel(chunk, filter_size, info, q_ref, ct_ref, x_ref, turned_ref, taps_ref, bias_ref, rim_ref, mask_ref,
                turned_mask_ref, sel_ref, order_ref, turned_order_ref, *rest):
    out_ref, gq_ref, gf_ref, conv_s, grad_s = rest[-5:]
    width = q_ref.shape[1]
    per = LANES // chunk
    steps = filter_size // TB
    depth = (steps + KINDS) * TB

    def one(sub, slot, further):
        lanes = pl.ds(pl.multiple_of(sub * LANES, LANES), LANES)
        bits, bits32 = chunk_bits(BF16, chunk), chunk_bits(F32, chunk)
        late, lane = TB - 1 - iota((TB, LANES), 0), iota((TB, LANES), 1)
        causal = lane % TB <= late
        rims = to_groups(rim_ref[:, lanes], bits, chunk)
        for g in range(per):
            at = sub * per + g
            xg = x_ref[at]
            ext = rims[g] + [xg[:, i : i + LANES] for i in range(0, xg.shape[1], LANES)]
            window = past_windows(ext, place_of(g, chunk), chunk, steps) + [xg] * (KINDS - 1)
            window = jnp.concatenate(window, axis=0) * mask_ref[g]
            y = jnp.dot(band_of(taps_ref[at])[:, :depth], window, preferred_element_type=F32)
            conv_s[slot, g] = chosen(y, sel_ref, g) + bias_ref[pl.ds(at, 1), :] * xg.astype(F32)
            turned = jnp.concatenate([turned_ref[at]] * KINDS, axis=0) * turned_mask_ref[g]
            pairs = lax.dot_general(turned, window, (((1,), (1,)), ((), ())), preferred_element_type=F32)
            pairs = jnp.concatenate([pairs, jnp.zeros((KINDS * TB, WIDE - depth), F32)], axis=1)
            far = pairs[(KINDS - 1) * TB :, :LANES]
            grad_s[slot, 0, g : g + 1, :] = skew_left(jnp.where(lane > late, far, 0.0))
            own = jnp.zeros((TB, LANES), F32)
            for kind in range(KINDS):
                first = (KINDS - 1 - kind) * TB
                own = jnp.where(causal & (lane // TB == kind), pairs[first : first + TB, LANES:], own)
            grad_s[slot, 1, g : g + 1, :] = skew_left(own)

        def more(index, carry):
            level, g = index // per, index % per
            at = sub * per + g
            here = order_ref[g] == level.astype(F32)
            xq = jnp.where(here, x_ref[at].astype(F32), 0.0).astype(BF16)
            turned = turned_order_ref[g] == level.astype(F32)
            turned = jnp.where(turned, turned_ref[at].astype(F32), 0.0).astype(BF16)
            own = taps_ref[at][TB : 2 * TB, :TB]
            conv_s[slot, g] += jnp.where(here, jnp.dot(own, xq, preferred_element_type=F32), 0.0)
            pairs = lax.dot_general(turned, xq, (((1,), (1,)), ((), ())), preferred_element_type=F32)
            pairs = jnp.concatenate([pairs, jnp.zeros((TB, LANES - TB), F32)], axis=1)
            grad_s[slot, 1, pl.ds(g, 1), :] += skew_left(jnp.where(causal & (lane < TB), pairs, 0.0))
            return carry

        if further:
            lax.fori_loop(KINDS * per, info[0] * per, more, 0)
        terms, own = grad_s[slot, 0], grad_s[slot, 1]
        last = iota((per, LANES), 1) >= LANES - TB
        for kind in range(KINDS):
            shift = (LANES - kind * TB) % LANES
            terms += jnp.where(last, pltpu.roll(own, shift, 1) if shift else own, 0.0)
        gf_ref[pl.ds(pl.multiple_of(sub * per, per), per), :] = terms
        filtered = from_groups([conv_s[slot, g] for g in range(per)], bits32, chunk)
        out_ref[:, lanes] = (q_ref[:, lanes].astype(F32) * filtered).astype(BF16)
        gq_ref[:, lanes] = (ct_ref[:, lanes].astype(F32) * filtered).astype(BF16)

    for_all_lanes(one, width // LANES, info)


def back_kernel(chunk, filter_size, info, k_ref, v_ref, dy_ref, taps_ref, bias_ref, rim_ref, mask_ref, sel_ref,
                order_ref, *rest):
    gk_ref, gv_ref, token_ref, back_s = rest[-4:]
    token_ref[...] = jnp.zeros_like(token_ref)
    width = k_ref.shape[1]
    per = LANES // chunk
    steps = filter_size // TB
    depth = (steps + KINDS) * TB

    def one(sub, slot, further):
        lanes = pl.ds(pl.multiple_of(sub * LANES, LANES), LANES)
        bits, bits32 = chunk_bits(BF16, chunk), chunk_bits(F32, chunk)
        rims = to_groups(rim_ref[:, lanes], bits, chunk)
        for g in range(per):
            at = sub * per + g
            dyg = dy_ref[at]
            ext = [dyg[:, i : i + LANES] for i in range(0, dyg.shape[1], LANES)] + rims[g]
            window = next_windows(ext, place_of(g, chunk), chunk, steps) + [dyg] * (KINDS - 1)
            window = jnp.concatenate(window, axis=0) * mask_ref[g]
            y = jnp.dot(band_of(taps_ref[at])[:, :depth], window, preferred_element_type=F32)
            back_s[slot, g] = chosen(y, sel_ref, g) + bias_ref[pl.ds(at, 1), :] * dyg.astype(F32)

        def more(index, carry):
            level, g = index // per, index % per
            at = sub * per + g
            here = order_ref[g] == level.astype(F32)
            dyq = jnp.where(here, dy_ref[at].astype(F32), 0.0).astype(BF16)
            own = taps_ref[at][:TB, :TB]
            back_s[slot, g] += jnp.where(here, jnp.dot(own, dyq, preferred_element_type=F32), 0.0)
            return carry

        if further:
            lax.fori_loop(KINDS * per, info[0] * per, more, 0)
        back = from_groups([back_s[slot, g] for g in range(per)], bits32, chunk)
        gk_ref[:, lanes] = (back * v_ref[:, lanes].astype(F32)).astype(BF16)
        gv_ref[:, lanes] = (back * k_ref[:, lanes].astype(F32)).astype(BF16)

    for_all_lanes(one, width // LANES, info)


def for_all_lanes(one, count, info):
    together = math.gcd(count, TOGETHER)

    def run(further):
        def step(index, carry):
            for slot in range(together):
                one(index * together + slot, slot, further)
            return carry

        lax.fori_loop(0, count // together, step, 0)

    pl.when(info[0] <= KINDS)(lambda: run(False))
    pl.when(info[0] > KINDS)(lambda: run(True))


def call(kernel, name, info, count, ins, outs, scratch=(), previous=None, after=()):
    operands = [a for a, _, _ in ins]
    in_specs = [pl.BlockSpec(block, at) for _, block, at in ins]
    aliases = {}
    if previous is not None:
        aliases = {1 + len(operands) + i: i for i in range(len(previous))}
        in_specs += [pl.BlockSpec(memory_space=pl.ANY)] * len(previous)
        operands += list(previous)
    in_specs += [pl.BlockSpec(memory_space=pl.ANY)] * len(after)
    operands += list(after)
    return pl.pallas_call(
        kernel,
        grid_spec=pltpu.PrefetchScalarGridSpec(
            num_scalar_prefetch=1,
            grid=(count,),
            in_specs=in_specs,
            out_specs=[pl.BlockSpec(block, at) for _, _, block, at in outs],
            scratch_shapes=list(scratch),
        ),
        out_shape=[jax.ShapeDtypeStruct(shape, kind) for shape, kind, _, _ in outs],
        input_output_aliases=aliases,
        compiler_params=pltpu.CompilerParams(vmem_limit_bytes=VMEM_BYTES),
        cost_estimate=pl.CostEstimate(flops=2**24, bytes_accessed=2**20, transcendentals=0),
        name=name,
    )(info, *operands)


def wide(array, block, first):
    return (array, (array.shape[0], block), lambda i, c: (0, first + i))


def per_group(array, groups, first):
    rest = array.shape[1:]
    return (array, (groups, *rest), lambda i, c: (first + i, *[0] * len(rest)))


def fixed(array):
    return (array, array.shape, lambda i, c: (0, 0, 0))


def prepare(info, big, filters):
    row_count, channels = big[0].shape
    chunk, block = TB, math.gcd(channels, 512)
    groups, total, filter_size = block // chunk, channels // chunk, filters.shape[1]
    taps = (filters, (groups, filter_size), lambda i, c: (c[0] * (channels // block) + i, 0))
    ins = [wide(a, block, 0) for a in big] + [taps]
    shapes = [(TB, row_count)] * 3 + [((1 + KINDS) * TB, LANES)] * 2
    outs = [((total, *s), BF16, (groups, *s), lambda i, c: (i, 0, 0)) for s in shapes]
    outs.append(((1, channels), F32, (1, block), lambda i, c: (0, i)))
    outs.append(((filter_size, channels), BF16, (filter_size, block), lambda i, c: (0, i)))
    return call(functools.partial(prepare_kernel, chunk), "prepare", info, channels // block, ins, outs)


def run_part(kernel, name, part, parts, info, pair, grouped, rim, rim_first, masks, filter_size, small, previous=None, after=()):
    row_count, channels = pair[0].shape
    chunk, width = TB, channels // parts
    block = math.gcd(width, 512)
    groups, first = block // chunk, part * (width // block)
    per = LANES // chunk
    ins = [wide(a, block, first) for a in pair] + [per_group(a, groups, first) for a in grouped]
    ins += [wide(rim, block, rim_first * (width // block))] + [fixed(a) for a in masks]
    outs = [((row_count, channels), BF16, (row_count, block), lambda i, c: (0, first + i))] * 2
    scratch = [pltpu.VMEM((TOGETHER, per, TB, row_count), F32)]
    if small:
        outs += [((channels // chunk, filter_size), F32, (groups, filter_size), lambda i, c: (first + i, 0))]
        scratch += [pltpu.VMEM((TOGETHER, 2, per, LANES), F32)]
    else:
        outs += [((8, LANES), F32, (8, LANES), lambda i, c: (0, 0))]
    kernel = functools.partial(kernel, chunk, filter_size)
    return call(kernel, name, info, width // block, ins, outs, scratch, previous, after)


def reset_kernel(steps, near_ref, mask_x, turned_x, sel_x, order_x, turned_order_x, mask_dy, sel_dy, order_dy, kinds):
    total = near_ref.shape[1]
    rows = total - steps * TB
    near = jnp.clip(near_ref[...], -1024, 1024).astype(F32)
    lane, row = iota((TB, total), 1), iota((TB, total), 0)
    spread = jnp.where(lane % TB == row, jnp.broadcast_to(near, (TB, total)), 0.0)
    same = flag(iota((total, total), 0) // TB == iota((total, total), 1) // TB, F32)
    begin = jnp.floor(exact_dot(spread, same) + 0.5)
    own = begin[:, :rows]
    block = iota((TB, rows), 1) // TB * TB
    pos = (block + iota((TB, rows), 0)).astype(F32)
    marks = flag((own == pos) & (iota((TB, rows), 0) > 0))
    before = flag(iota((TB, TB), 0) >= iota((TB, TB), 1))
    order = jnp.dot(before, marks, preferred_element_type=F32)
    behind = order[TB - 1 :] - order
    first = jnp.broadcast_to(own[:1], (TB, rows))
    turn = permutation(TB)

    def put(ref, at, value):
        parts = [value[:, i : i + LANES] for i in range(0, rows, LANES)]
        for g in range(ref.shape[0]):
            turned = side_by_side([pltpu.roll(a, g * TB, 1) if g else a for a in parts])
            ref[g, at * TB : (at + 1) * TB, :] = turned.astype(ref.dtype)

    for i in range(steps):
        put(mask_x, i, flag(pos - TB * (steps - i) >= first, F32))
        later = pltpu.roll(begin, total - (i + 1) * TB, 1)[:, :rows]
        put(mask_dy, i + 1, flag(later <= (block + TB - 1).astype(F32), F32))
    for kind in range(KINDS):
        put(mask_x, steps + kind, flag(order == kind, F32))
        put(sel_x, kind, flag(order == kind, F32))
        put(turned_x, KINDS - 1 - kind, jnp.dot(turn, flag(order == kind), preferred_element_type=F32))
        put(mask_dy, steps + kind if kind else 0, flag(behind == kind, F32))
        put(sel_dy, kind, flag(behind == kind, F32))
    put(order_x, 0, order)
    put(order_dy, 0, behind)
    put(turned_order_x, 0, jnp.dot(turn, order.astype(BF16), preferred_element_type=F32))
    kinds[0] = 1 + jnp.max(order).astype(jnp.int32)


def reset_masks(near, row_count, steps):
    depth, high, per = (steps + KINDS) * TB, KINDS * TB, LANES // TB
    shapes = [(depth, BF16), (high, BF16), (high, F32), (TB, F32), (TB, F32), (depth, BF16), (high, F32), (TB, F32)]
    out = pl.pallas_call(
        functools.partial(reset_kernel, steps),
        out_shape=[jax.ShapeDtypeStruct((per, rows, row_count), kind) for rows, kind in shapes]
        + [jax.ShapeDtypeStruct((1,), jnp.int32)],
        out_specs=[pl.BlockSpec(memory_space=pltpu.VMEM)] * len(shapes) + [pl.BlockSpec(memory_space=pltpu.SMEM)],
        compiler_params=pltpu.CompilerParams(vmem_limit_bytes=VMEM_BYTES),
        name="resets",
    )(near)
    return out[:5], out[5:8], out[8]


def passed_along(value, axis, steps):
    count = lax.axis_size(axis)
    initial, last = (max(0, -steps), min(count, count - steps))
    return lax.ppermute(value, axis, [(source, source + steps) for source in range(initial, last)])


def doubling(value, axis):
    count = lax.axis_size(axis)
    if count & (count - 1):
        yield [value, lax.psum(value, axis)]
        return
    step = 1
    while step < count:
        state = [lax.ppermute(value, axis, [(i, i ^ step) for i in range(count)]), value]
        yield state
        value = state[1] = state[0] + value
        step *= 2
    yield [value, value]


def rows_of_all(value, axis):
    count = lax.axis_size(axis)
    if count != 2:
        return lax.all_gather(value, axis, axis=0, tiled=True)
    other = lax.ppermute(value, axis, [(0, 1), (1, 0)])
    is_first = lax.axis_index(axis) == 0
    return jnp.concatenate([jnp.where(is_first, value, other), jnp.where(is_first, other, value)], axis=0)


def body(queries, key_branch, value_branch, cotangent, filters, skip_bias, contig_start):
    row_count, channels = queries.shape
    group_total, filter_size = filters.shape
    ctx_count, tp_count = lax.axis_size("ctx"), lax.axis_size("tp")
    shard, tensor = lax.axis_index("ctx"), lax.axis_index("tp")
    token_count = row_count * ctx_count
    chunk = channels * tp_count // group_total
    groups = channels // chunk

    tail = lambda m: m[row_count - filter_size :]
    left = passed_along(product_bf16(tail(key_branch), tail(value_branch)), "ctx", 1)

    starts = jnp.concatenate([contig_start, jnp.full((filter_size,), 2**30, jnp.int32)])
    first = shard * row_count
    near = (lax.dynamic_slice_in_dim(starts, first, row_count + filter_size, 0) - first)[None, :]
    masks_x, masks_dy, kinds = reset_masks(near, row_count, filter_size // TB)
    bias = jnp.tile(skip_bias.reshape(groups, chunk), (1, row_count // TB))
    big = (queries, cotangent, key_branch, value_branch)
    place = tensor.astype(jnp.int32).reshape(1)
    place, kinds, bias = lax.optimization_barrier((place, kinds, bias))
    x, dy, turned, band_x, band_dy, bias_part, head = prepare(place, big, filters)

    left, head = lax.optimization_barrier((left, head))
    right = passed_along(head, "ctx", -1)

    pair, grouped = (queries, cotangent), (x, turned, band_x, bias)
    output, grad_query, filter_part = run_part(
        conv_kernel, "conv", 0, 1, kinds, pair, grouped, left, 0, masks_x, filter_size, True
    )
    terms = jnp.concatenate([filter_part, bias_part.reshape(channels // filter_size, filter_size)], axis=0)

    pair, grouped = (key_branch, value_branch), (dy, band_dy, bias)
    sums = doubling(terms, "ctx")
    done, after, state = None, (), None
    for part in range(BACK_PARTS):
        arriving = next(sums, None)
        state = arriving or state
        *done, token = run_part(
            back_kernel, "back", part, BACK_PARTS, kinds, pair, grouped, right, part, masks_dy, filter_size, False, done, after
        )
        if arriving is not None:
            arriving[0], token = lax.optimization_barrier((arriving[0], token))
        after = (token,)
    grad_key, grad_value = done
    for state in sums:
        pass
    terms = state[1]
    grad_filter = rows_of_all(terms[:groups], "tp")[:, ::-1] * (1.0 / math.sqrt(token_count * chunk))
    grad_bias = terms[groups:].reshape(channels) * (1.0 / math.sqrt(token_count))
    return (output, grad_query, grad_key, grad_value, grad_filter, grad_bias)


def solution(mesh):
    whole = P("ctx", "tp")
    return jax.shard_map(
        body,
        mesh=mesh,
        in_specs=(whole, whole, whole, whole, P(), P("tp"), P()),
        out_specs=(whole, whole, whole, whole, P(), P("tp")),
        check_vma=False,
    )
```

```python
import functools
import math

import jax
import jax.numpy as jnp
from jax import lax
from jax.experimental import pallas as pl
from jax.experimental.pallas import tpu as pltpu
from jax.sharding import PartitionSpec as P

F32, BF16 = jnp.float32, jnp.bfloat16
LANES = 128
TB = 16
WIDE = 256
KINDS = 3
BACK_PARTS = 2
VMEM_BYTES = 60 * 1024 * 1024
TOGETHER = 2


def iota(shape, axis):
    return lax.broadcasted_iota(jnp.int32, shape, axis)


def flag(condition, kind=BF16):
    return jnp.where(condition, 1.0, 0.0).astype(kind)


def permutation(size):
    return flag(iota((size, size), 0) + iota((size, size), 1) == size - 1)


def chunk_of(shape, kind, chunk):
    return (iota(shape, 1) // chunk).astype(F32).astype(kind)


def swap_chunks(arrays, bits):
    count = len(arrays)
    rows = [arrays[(-i) % count] for i in range(count)]
    for power, moved in enumerate(bits):
        bit = 1 << power
        rows = [jnp.where(moved, rows[(i - bit) % count], rows[i]) for i in range(count)]
    return rows


def chunk_bits(kind, chunk):
    pos = iota((TB, LANES), 1) // chunk
    return [flag((pos >> power) & 1 == 1, kind) > 0 for power in range((LANES // chunk).bit_length() - 1)]


def to_groups(block, bits, chunk):
    per = LANES // chunk
    sets = []
    for first in range(0, block.shape[0], TB * per):
        parts = [block[first + TB * n : first + TB * (n + 1)] for n in range(per)]
        sets.append(swap_chunks([pltpu.roll(a, n * chunk, 1) if n else a for n, a in enumerate(parts)], bits))
    return [[s[g] for s in sets] for g in range(per)]


def from_groups(chunked, bits, chunk):
    rows = []
    for first in range(0, chunked[0].shape[1], LANES):
        parts = swap_chunks([a[:, first : first + LANES] for a in chunked], bits)
        rows += [pltpu.roll(a, LANES - n * chunk, 1) if n else a for n, a in enumerate(parts)]
    return jnp.concatenate(rows, axis=0)


def place_of(g, chunk):
    per = LANES // chunk
    return ((iota((TB, LANES), 1) // chunk + per - g) % per).astype(F32).astype(BF16)


def past_windows(ext, place, chunk, count):
    per = LANES // chunk
    out = []
    for back in range(count, -1, -1):
        whole, part = divmod(back, per)
        width = len(ext) - count // per
        vregs = []
        for v in range(width):
            near = len(ext) - width + v - whole
            if part:
                vregs.append(pltpu.roll(jnp.where(place < per - part, ext[near], ext[near - 1]), part * chunk, 1))
            else:
                vregs.append(ext[near])
        out.append(side_by_side(vregs))
    return out


def next_windows(ext, place, chunk, count):
    per = LANES // chunk
    width = len(ext) - count // per
    out = []
    for ahead in range(count + 1):
        whole, part = divmod(ahead, per)
        vregs = []
        for v in range(width):
            near = v + whole
            if part:
                vregs.append(pltpu.roll(jnp.where(place >= part, ext[near], ext[near + 1]), LANES - part * chunk, 1))
            else:
                vregs.append(ext[near])
        out.append(side_by_side(vregs))
    return out


def side_by_side(vregs):
    return vregs[0] if len(vregs) == 1 else jnp.concatenate(vregs, axis=1)


def product_bf16(a, b):
    return (a.astype(F32) * b.astype(F32)).astype(BF16)


def skew_left(products):
    moved = pltpu.roll(products, LANES - TB, 1, stride=1, stride_axis=0)
    return jnp.sum(moved, axis=0, keepdims=True)


def exact_dot(a, b):
    return jnp.dot(a, b, precision=lax.Precision.HIGHEST, preferred_element_type=F32)


def shifted_taps(row, first):
    base = jnp.concatenate([row, jnp.zeros((1, WIDE - row.shape[1]), F32)], axis=1)
    base = jnp.broadcast_to(base, (TB, WIDE))
    return pltpu.roll(base, first, 1, stride=1, stride_axis=0).astype(BF16)


def chosen(products, sel_ref, g, kinds):
    return sum(
        products[kind * TB : (kind + 1) * TB] * sel_ref[g, kind * TB : (kind + 1) * TB, :] for kind in range(kinds)
    )


def with_kinds(taps, own, chunk):
    pos = chunk_of((TB, LANES), BF16, chunk)
    zero = jnp.zeros((TB, LANES), BF16)
    further = [jnp.where(pos == kind, pltpu.roll(own, kind * TB, 1), zero) for kind in range(1, KINDS)]
    return jnp.concatenate([taps[:, :LANES], taps[:, LANES:]] + further, axis=0)


def band_of(stored, kinds):
    none = jnp.zeros(((kinds - 1) * TB, LANES), BF16)
    return jnp.concatenate([jnp.concatenate([stored[:TB], none], axis=0), stored[TB : (1 + kinds) * TB]], axis=1)


def prepare_kernel(chunk, info, q_ref, ct_ref, k_ref, v_ref, taps_ref, x_ref, dy_ref, turned_ref, bx_ref, bdy_ref, gb_ref, head_ref):
    width = q_ref.shape[1]
    filter_size = taps_ref.shape[1]
    per = LANES // chunk
    for sub in range(width // LANES):
        lanes = pl.ds(sub * LANES, LANES)
        bits = chunk_bits(BF16, chunk)
        x = product_bf16(k_ref[:, lanes], v_ref[:, lanes])
        dy = product_bf16(ct_ref[:, lanes], q_ref[:, lanes])
        gb_ref[:, lanes] = jnp.sum(x.astype(F32) * dy.astype(F32), axis=0, keepdims=True)
        head_ref[:, lanes] = dy[:filter_size]
        xs, dys = to_groups(x, bits, chunk), to_groups(dy, bits, chunk)
        taps = taps_ref[pl.ds(sub * per, per), :]
        back = jnp.dot(taps.astype(BF16), permutation(filter_size), preferred_element_type=F32)
        for g in range(per):
            at = sub * per + g
            x_ref[at] = side_by_side(xs[g])
            dyg = side_by_side(dys[g])
            dy_ref[at] = dyg
            turned_ref[at] = jnp.dot(permutation(TB), dyg, preferred_element_type=F32).astype(BF16)
            band = shifted_taps(back[g : g + 1], 1)
            bx_ref[at] = with_kinds(band, band[:, LANES:], chunk)
            band = shifted_taps(taps[g : g + 1], 0)
            bdy_ref[at] = with_kinds(band, band[:, :LANES], chunk)


def conv_kernel(chunk, filter_size, info, q_ref, ct_ref, x_ref, turned_ref, taps_ref, bias_ref, rim_ref, mask_ref,
                turned_mask_ref, sel_ref, order_ref, turned_order_ref, *rest):
    out_ref, gq_ref, gf_ref, conv_s, grad_s = rest[-5:]
    width = q_ref.shape[1]
    per = LANES // chunk
    steps = filter_size // TB

    def one(sub, slot, kinds, further):
        depth = (steps + kinds) * TB
        lanes = pl.ds(pl.multiple_of(sub * LANES, LANES), LANES)
        bits, bits32 = chunk_bits(BF16, chunk), chunk_bits(F32, chunk)
        late, lane = TB - 1 - iota((TB, LANES), 0), iota((TB, LANES), 1)
        causal = lane % TB <= late
        rims = to_groups(rim_ref[:, lanes], bits, chunk)
        for g in range(per):
            at = sub * per + g
            xg = x_ref[at]
            ext = rims[g] + [xg[:, i : i + LANES] for i in range(0, xg.shape[1], LANES)]
            window = past_windows(ext, place_of(g, chunk), chunk, steps) + [xg] * (kinds - 1)
            window = jnp.concatenate(window, axis=0) * mask_ref[g, :depth, :]
            y = jnp.dot(band_of(taps_ref[at], kinds)[:, :depth], window, preferred_element_type=F32)
            conv_s[slot, g] = chosen(y, sel_ref, g, kinds) + bias_ref[pl.ds(at, 1), :] * xg.astype(F32)
            turned = jnp.concatenate([turned_ref[at]] * kinds, axis=0) * turned_mask_ref[g, (KINDS - kinds) * TB :, :]
            pairs = lax.dot_general(turned, window, (((1,), (1,)), ((), ())), preferred_element_type=F32)
            pairs = jnp.concatenate([pairs, jnp.zeros((kinds * TB, WIDE - depth), F32)], axis=1)
            far = pairs[(kinds - 1) * TB :, :LANES]
            grad_s[slot, 0, g : g + 1, :] = skew_left(jnp.where(lane > late, far, 0.0))
            own = jnp.zeros((TB, LANES), F32)
            for kind in range(kinds):
                first = (kinds - 1 - kind) * TB
                own = jnp.where(causal & (lane // TB == kind), pairs[first : first + TB, LANES:], own)
            grad_s[slot, 1, g : g + 1, :] = skew_left(own)

        def more(index, carry):
            level, g = index // per, index % per
            at = sub * per + g
            here = order_ref[g] == level.astype(F32)
            xq = jnp.where(here, x_ref[at].astype(F32), 0.0).astype(BF16)
            turned = turned_order_ref[g] == level.astype(F32)
            turned = jnp.where(turned, turned_ref[at].astype(F32), 0.0).astype(BF16)
            own = taps_ref[at][TB : 2 * TB, :TB]
            conv_s[slot, g] += jnp.where(here, jnp.dot(own, xq, preferred_element_type=F32), 0.0)
            pairs = lax.dot_general(turned, xq, (((1,), (1,)), ((), ())), preferred_element_type=F32)
            pairs = jnp.concatenate([pairs, jnp.zeros((TB, LANES - TB), F32)], axis=1)
            grad_s[slot, 1, pl.ds(g, 1), :] += skew_left(jnp.where(causal & (lane < TB), pairs, 0.0))
            return carry

        if further:
            lax.fori_loop(KINDS * per, info[0] * per, more, 0)
        terms, own = grad_s[slot, 0], grad_s[slot, 1]
        last = iota((per, LANES), 1) >= LANES - TB
        for kind in range(kinds):
            shift = (LANES - kind * TB) % LANES
            terms += jnp.where(last, pltpu.roll(own, shift, 1) if shift else own, 0.0)
        gf_ref[pl.ds(pl.multiple_of(sub * per, per), per), :] = terms
        filtered = from_groups([conv_s[slot, g] for g in range(per)], bits32, chunk)
        out_ref[:, lanes] = (q_ref[:, lanes].astype(F32) * filtered).astype(BF16)
        gq_ref[:, lanes] = (ct_ref[:, lanes].astype(F32) * filtered).astype(BF16)

    for_all_lanes(one, width // LANES, info)


def back_kernel(chunk, filter_size, info, k_ref, v_ref, dy_ref, taps_ref, bias_ref, rim_ref, mask_ref, sel_ref,
                order_ref, *rest):
    gk_ref, gv_ref, token_ref, back_s = rest[-4:]
    token_ref[...] = jnp.zeros_like(token_ref)
    width = k_ref.shape[1]
    per = LANES // chunk
    steps = filter_size // TB

    def one(sub, slot, kinds, further):
        depth = (steps + kinds) * TB
        lanes = pl.ds(pl.multiple_of(sub * LANES, LANES), LANES)
        bits, bits32 = chunk_bits(BF16, chunk), chunk_bits(F32, chunk)
        rims = to_groups(rim_ref[:, lanes], bits, chunk)
        for g in range(per):
            at = sub * per + g
            dyg = dy_ref[at]
            ext = [dyg[:, i : i + LANES] for i in range(0, dyg.shape[1], LANES)] + rims[g]
            window = next_windows(ext, place_of(g, chunk), chunk, steps) + [dyg] * (kinds - 1)
            window = jnp.concatenate(window, axis=0) * mask_ref[g, :depth, :]
            y = jnp.dot(band_of(taps_ref[at], kinds)[:, :depth], window, preferred_element_type=F32)
            back_s[slot, g] = chosen(y, sel_ref, g, kinds) + bias_ref[pl.ds(at, 1), :] * dyg.astype(F32)

        def more(index, carry):
            level, g = index // per, index % per
            at = sub * per + g
            here = order_ref[g] == level.astype(F32)
            dyq = jnp.where(here, dy_ref[at].astype(F32), 0.0).astype(BF16)
            own = taps_ref[at][:TB, :TB]
            back_s[slot, g] += jnp.where(here, jnp.dot(own, dyq, preferred_element_type=F32), 0.0)
            return carry

        if further:
            lax.fori_loop(KINDS * per, info[0] * per, more, 0)
        back = from_groups([back_s[slot, g] for g in range(per)], bits32, chunk)
        gk_ref[:, lanes] = (back * v_ref[:, lanes].astype(F32)).astype(BF16)
        gv_ref[:, lanes] = (back * k_ref[:, lanes].astype(F32)).astype(BF16)

    for_all_lanes(one, width // LANES, info)


def for_all_lanes(one, count, info):
    together = math.gcd(count, TOGETHER)

    def run(kinds, further):
        def step(index, carry):
            for slot in range(together):
                one(index * together + slot, slot, kinds, further)
            return carry

        lax.fori_loop(0, count // together, step, 0)

    pl.when(info[0] < KINDS)(lambda: run(KINDS - 1, False))
    pl.when(info[0] == KINDS)(lambda: run(KINDS, False))
    pl.when(info[0] > KINDS)(lambda: run(KINDS, True))


def call(kernel, name, info, count, ins, outs, scratch=(), previous=None, after=()):
    operands = [a for a, _, _ in ins]
    in_specs = [pl.BlockSpec(block, at) for _, block, at in ins]
    aliases = {}
    if previous is not None:
        aliases = {1 + len(operands) + i: i for i in range(len(previous))}
        in_specs += [pl.BlockSpec(memory_space=pl.ANY)] * len(previous)
        operands += list(previous)
    in_specs += [pl.BlockSpec(memory_space=pl.ANY)] * len(after)
    operands += list(after)
    return pl.pallas_call(
        kernel,
        grid_spec=pltpu.PrefetchScalarGridSpec(
            num_scalar_prefetch=1,
            grid=(count,),
            in_specs=in_specs,
            out_specs=[pl.BlockSpec(block, at) for _, _, block, at in outs],
            scratch_shapes=list(scratch),
        ),
        out_shape=[jax.ShapeDtypeStruct(shape, kind) for shape, kind, _, _ in outs],
        input_output_aliases=aliases,
        compiler_params=pltpu.CompilerParams(vmem_limit_bytes=VMEM_BYTES),
        cost_estimate=pl.CostEstimate(flops=2**24, bytes_accessed=2**20, transcendentals=0),
        name=name,
    )(info, *operands)


def wide(array, block, first):
    return (array, (array.shape[0], block), lambda i, c: (0, first + i))


def per_group(array, groups, first):
    rest = array.shape[1:]
    return (array, (groups, *rest), lambda i, c: (first + i, *[0] * len(rest)))


def fixed(array):
    return (array, array.shape, lambda i, c: (0, 0, 0))


def prepare(info, big, filters):
    row_count, channels = big[0].shape
    chunk, block = TB, math.gcd(channels, 512)
    groups, total, filter_size = block // chunk, channels // chunk, filters.shape[1]
    taps = (filters, (groups, filter_size), lambda i, c: (c[0] * (channels // block) + i, 0))
    ins = [wide(a, block, 0) for a in big] + [taps]
    shapes = [(TB, row_count)] * 3 + [((1 + KINDS) * TB, LANES)] * 2
    outs = [((total, *s), BF16, (groups, *s), lambda i, c: (i, 0, 0)) for s in shapes]
    outs.append(((1, channels), F32, (1, block), lambda i, c: (0, i)))
    outs.append(((filter_size, channels), BF16, (filter_size, block), lambda i, c: (0, i)))
    return call(functools.partial(prepare_kernel, chunk), "prepare", info, channels // block, ins, outs)


def run_part(kernel, name, part, parts, info, pair, grouped, rim, rim_first, masks, filter_size, small, previous=None, after=()):
    row_count, channels = pair[0].shape
    chunk, width = TB, channels // parts
    block = math.gcd(width, 512)
    groups, first = block // chunk, part * (width // block)
    per = LANES // chunk
    ins = [wide(a, block, first) for a in pair] + [per_group(a, groups, first) for a in grouped]
    ins += [wide(rim, block, rim_first * (width // block))] + [fixed(a) for a in masks]
    outs = [((row_count, channels), BF16, (row_count, block), lambda i, c: (0, first + i))] * 2
    scratch = [pltpu.VMEM((TOGETHER, per, TB, row_count), F32)]
    if small:
        outs += [((channels // chunk, filter_size), F32, (groups, filter_size), lambda i, c: (first + i, 0))]
        scratch += [pltpu.VMEM((TOGETHER, 2, per, LANES), F32)]
    else:
        outs += [((8, LANES), F32, (8, LANES), lambda i, c: (0, 0))]
    kernel = functools.partial(kernel, chunk, filter_size)
    return call(kernel, name, info, width // block, ins, outs, scratch, previous, after)


def reset_kernel(steps, near_ref, mask_x, turned_x, sel_x, order_x, turned_order_x, mask_dy, sel_dy, order_dy, kinds):
    total = near_ref.shape[1]
    rows = total - steps * TB
    near = jnp.clip(near_ref[...], -1024, 1024).astype(F32)
    lane, row = iota((TB, total), 1), iota((TB, total), 0)
    spread = jnp.where(lane % TB == row, jnp.broadcast_to(near, (TB, total)), 0.0)
    same = flag(iota((total, total), 0) // TB == iota((total, total), 1) // TB, F32)
    begin = jnp.floor(exact_dot(spread, same) + 0.5)
    own = begin[:, :rows]
    block = iota((TB, rows), 1) // TB * TB
    pos = (block + iota((TB, rows), 0)).astype(F32)
    marks = flag((own == pos) & (iota((TB, rows), 0) > 0))
    before = flag(iota((TB, TB), 0) >= iota((TB, TB), 1))
    order = jnp.dot(before, marks, preferred_element_type=F32)
    behind = order[TB - 1 :] - order
    first = jnp.broadcast_to(own[:1], (TB, rows))
    turn = permutation(TB)

    def put(ref, at, value):
        parts = [value[:, i : i + LANES] for i in range(0, rows, LANES)]
        for g in range(ref.shape[0]):
            turned = side_by_side([pltpu.roll(a, g * TB, 1) if g else a for a in parts])
            ref[g, at * TB : (at + 1) * TB, :] = turned.astype(ref.dtype)

    for i in range(steps):
        put(mask_x, i, flag(pos - TB * (steps - i) >= first, F32))
        later = pltpu.roll(begin, total - (i + 1) * TB, 1)[:, :rows]
        put(mask_dy, i + 1, flag(later <= (block + TB - 1).astype(F32), F32))
    for kind in range(KINDS):
        put(mask_x, steps + kind, flag(order == kind, F32))
        put(sel_x, kind, flag(order == kind, F32))
        put(turned_x, KINDS - 1 - kind, jnp.dot(turn, flag(order == kind), preferred_element_type=F32))
        put(mask_dy, steps + kind if kind else 0, flag(behind == kind, F32))
        put(sel_dy, kind, flag(behind == kind, F32))
    put(order_x, 0, order)
    put(order_dy, 0, behind)
    put(turned_order_x, 0, jnp.dot(turn, order.astype(BF16), preferred_element_type=F32))
    kinds[0] = 1 + jnp.max(order).astype(jnp.int32)


def reset_masks(near, row_count, steps):
    depth, high, per = (steps + KINDS) * TB, KINDS * TB, LANES // TB
    shapes = [(depth, BF16), (high, BF16), (high, F32), (TB, F32), (TB, F32), (depth, BF16), (high, F32), (TB, F32)]
    out = pl.pallas_call(
        functools.partial(reset_kernel, steps),
        out_shape=[jax.ShapeDtypeStruct((per, rows, row_count), kind) for rows, kind in shapes]
        + [jax.ShapeDtypeStruct((1,), jnp.int32)],
        out_specs=[pl.BlockSpec(memory_space=pltpu.VMEM)] * len(shapes) + [pl.BlockSpec(memory_space=pltpu.SMEM)],
        compiler_params=pltpu.CompilerParams(vmem_limit_bytes=VMEM_BYTES),
        name="resets",
    )(near)
    return out[:5], out[5:8], out[8]


def passed_along(value, axis, steps):
    count = lax.axis_size(axis)
    initial, last = (max(0, -steps), min(count, count - steps))
    return lax.ppermute(value, axis, [(source, source + steps) for source in range(initial, last)])


def rounds_of_sum(value, axis):
    count = lax.axis_size(axis)
    if count & (count - 1):
        yield [[value], lax.psum(value, axis)]
        return
    step = 1
    while step < count:
        flips = [step] if 2 * step == count else [step, 2 * step, 3 * step]
        state = [[lax.ppermute(value, axis, [(i, i ^ flip) for i in range(count)]) for flip in flips], value]
        yield state
        near, *far = state[0]
        value = value + near
        if far:
            value = value + (far[0] + far[1])
        state[1] = value
        step <<= len(flips).bit_length()
    yield [[value], value]


def rows_of_all(value, axis):
    count = lax.axis_size(axis)
    if count != 2:
        return lax.all_gather(value, axis, axis=0, tiled=True)
    other = lax.ppermute(value, axis, [(0, 1), (1, 0)])
    is_first = lax.axis_index(axis) == 0
    return jnp.concatenate([jnp.where(is_first, value, other), jnp.where(is_first, other, value)], axis=0)


def body(queries, key_branch, value_branch, cotangent, filters, skip_bias, contig_start):
    row_count, channels = queries.shape
    group_total, filter_size = filters.shape
    ctx_count, tp_count = lax.axis_size("ctx"), lax.axis_size("tp")
    shard, tensor = lax.axis_index("ctx"), lax.axis_index("tp")
    token_count = row_count * ctx_count
    chunk = channels * tp_count // group_total
    groups = channels // chunk

    tail = lambda m: m[row_count - filter_size :]
    left = passed_along(product_bf16(tail(key_branch), tail(value_branch)), "ctx", 1)

    starts = jnp.concatenate([contig_start, jnp.full((filter_size,), 2**30, jnp.int32)])
    first = shard * row_count
    near = (lax.dynamic_slice_in_dim(starts, first, row_count + filter_size, 0) - first)[None, :]
    masks_x, masks_dy, kinds = reset_masks(near, row_count, filter_size // TB)
    bias = jnp.tile(skip_bias.reshape(groups, chunk), (1, row_count // TB))
    big = (queries, cotangent, key_branch, value_branch)
    place = tensor.astype(jnp.int32).reshape(1)
    place, kinds, bias = lax.optimization_barrier((place, kinds, bias))
    x, dy, turned, band_x, band_dy, bias_part, head = prepare(place, big, filters)

    left, head = lax.optimization_barrier((left, head))
    right = passed_along(head, "ctx", -1)

    pair, grouped = (queries, cotangent), (x, turned, band_x, bias)
    output, grad_query, filter_part = run_part(
        conv_kernel, "conv", 0, 1, kinds, pair, grouped, left, 0, masks_x, filter_size, True
    )
    terms = jnp.concatenate([filter_part, bias_part.reshape(channels // filter_size, filter_size)], axis=0)

    pair, grouped = (key_branch, value_branch), (dy, band_dy, bias)
    sums = rounds_of_sum(terms, "ctx")
    done, after, state = None, (), None
    for part in range(BACK_PARTS):
        arriving = next(sums, None)
        state = arriving or state
        *done, token = run_part(
            back_kernel, "back", part, BACK_PARTS, kinds, pair, grouped, right, part, masks_dy, filter_size, False, done, after
        )
        if arriving is not None:
            *arriving[0], token = lax.optimization_barrier((*arriving[0], token))
        after = (token,)
    grad_key, grad_value = done
    for state in sums:
        pass
    terms = state[1]
    grad_filter = rows_of_all(terms[:groups], "tp")[:, ::-1] * (1.0 / math.sqrt(token_count * chunk))
    grad_bias = terms[groups:].reshape(channels) * (1.0 / math.sqrt(token_count))
    return (output, grad_query, grad_key, grad_value, grad_filter, grad_bias)


def solution(mesh):
    whole = P("ctx", "tp")
    return jax.shard_map(
        body,
        mesh=mesh,
        in_specs=(whole, whole, whole, whole, P(), P("tp"), P()),
        out_specs=(whole, whole, whole, whole, P(), P("tp")),
        check_vma=False,
    )
```

```python
import functools
import math

import jax
import jax.numpy as jnp
from jax import lax
from jax.experimental import pallas as pl
from jax.experimental.pallas import tpu as pltpu
from jax.sharding import PartitionSpec as P

F32, BF16 = jnp.float32, jnp.bfloat16
LANES = 128
TB = 16
WIDE = 256
KINDS = 3
BACK_PARTS = 2
VMEM_BYTES = 60 * 1024 * 1024
TOGETHER = 4


def iota(shape, axis):
    return lax.broadcasted_iota(jnp.int32, shape, axis)


def flag(condition, kind=BF16):
    return jnp.where(condition, 1.0, 0.0).astype(kind)


def permutation(size):
    return flag(iota((size, size), 0) + iota((size, size), 1) == size - 1)


def chunk_of(shape, kind, chunk):
    return (iota(shape, 1) // chunk).astype(F32).astype(kind)


def swap_chunks(arrays, bits):
    count = len(arrays)
    rows = [arrays[(-i) % count] for i in range(count)]
    for power, moved in enumerate(bits):
        bit = 1 << power
        rows = [jnp.where(moved, rows[(i - bit) % count], rows[i]) for i in range(count)]
    return rows


def chunk_bits(kind, chunk):
    pos = iota((TB, LANES), 1) // chunk
    return [flag((pos >> power) & 1 == 1, kind) > 0 for power in range((LANES // chunk).bit_length() - 1)]


def to_groups(block, bits, chunk):
    per = LANES // chunk
    sets = []
    for first in range(0, block.shape[0], TB * per):
        parts = [block[first + TB * n : first + TB * (n + 1)] for n in range(per)]
        sets.append(swap_chunks([pltpu.roll(a, n * chunk, 1) if n else a for n, a in enumerate(parts)], bits))
    return [[s[g] for s in sets] for g in range(per)]


def from_groups(chunked, bits, chunk):
    rows = []
    for first in range(0, chunked[0].shape[1], LANES):
        parts = swap_chunks([a[:, first : first + LANES] for a in chunked], bits)
        rows += [pltpu.roll(a, LANES - n * chunk, 1) if n else a for n, a in enumerate(parts)]
    return jnp.concatenate(rows, axis=0)


def place_of(g, chunk):
    per = LANES // chunk
    return ((iota((TB, LANES), 1) // chunk + per - g) % per).astype(F32).astype(BF16)


def past_windows(ext, place, chunk, count):
    per = LANES // chunk
    out = []
    for back in range(count, -1, -1):
        whole, part = divmod(back, per)
        width = len(ext) - count // per
        vregs = []
        for v in range(width):
            near = len(ext) - width + v - whole
            if part:
                vregs.append(pltpu.roll(jnp.where(place < per - part, ext[near], ext[near - 1]), part * chunk, 1))
            else:
                vregs.append(ext[near])
        out.append(side_by_side(vregs))
    return out


def next_windows(ext, place, chunk, count):
    per = LANES // chunk
    width = len(ext) - count // per
    out = []
    for ahead in range(count + 1):
        whole, part = divmod(ahead, per)
        vregs = []
        for v in range(width):
            near = v + whole
            if part:
                vregs.append(pltpu.roll(jnp.where(place >= part, ext[near], ext[near + 1]), LANES - part * chunk, 1))
            else:
                vregs.append(ext[near])
        out.append(side_by_side(vregs))
    return out


def side_by_side(vregs):
    return vregs[0] if len(vregs) == 1 else jnp.concatenate(vregs, axis=1)


def product_bf16(a, b):
    return (a.astype(F32) * b.astype(F32)).astype(BF16)


def skew_left(products):
    moved = pltpu.roll(products, LANES - TB, 1, stride=1, stride_axis=0)
    return jnp.sum(moved, axis=0, keepdims=True)


def exact_dot(a, b):
    return jnp.dot(a, b, precision=lax.Precision.HIGHEST, preferred_element_type=F32)


def shifted_taps(row, first):
    base = jnp.concatenate([row, jnp.zeros((1, WIDE - row.shape[1]), F32)], axis=1)
    base = jnp.broadcast_to(base, (TB, WIDE))
    return pltpu.roll(base, first, 1, stride=1, stride_axis=0).astype(BF16)


def chosen(products, sel_ref, g, kinds):
    return sum(
        products[kind * TB : (kind + 1) * TB] * sel_ref[g, kind * TB : (kind + 1) * TB, :] for kind in range(kinds)
    )


def with_kinds(taps, own, chunk):
    pos = chunk_of((TB, LANES), BF16, chunk)
    zero = jnp.zeros((TB, LANES), BF16)
    further = [jnp.where(pos == kind, pltpu.roll(own, kind * TB, 1), zero) for kind in range(1, KINDS)]
    return jnp.concatenate([taps[:, :LANES], taps[:, LANES:]] + further, axis=0)


def band_of(stored, kinds):
    none = jnp.zeros(((kinds - 1) * TB, LANES), BF16)
    return jnp.concatenate([jnp.concatenate([stored[:TB], none], axis=0), stored[TB : (1 + kinds) * TB]], axis=1)


def prepare_kernel(chunk, info, q_ref, ct_ref, k_ref, v_ref, taps_ref, x_ref, dy_ref, turned_ref, bx_ref, bdy_ref, gb_ref, head_ref):
    width = q_ref.shape[1]
    filter_size = taps_ref.shape[1]
    per = LANES // chunk
    for sub in range(width // LANES):
        lanes = pl.ds(sub * LANES, LANES)
        bits = chunk_bits(BF16, chunk)
        x = product_bf16(k_ref[:, lanes], v_ref[:, lanes])
        dy = product_bf16(ct_ref[:, lanes], q_ref[:, lanes])
        gb_ref[:, lanes] = jnp.sum(x.astype(F32) * dy.astype(F32), axis=0, keepdims=True)
        head_ref[:, lanes] = dy[:filter_size]
        xs, dys = to_groups(x, bits, chunk), to_groups(dy, bits, chunk)
        taps = taps_ref[pl.ds(sub * per, per), :]
        back = jnp.dot(taps.astype(BF16), permutation(filter_size), preferred_element_type=F32)
        for g in range(per):
            at = sub * per + g
            x_ref[at] = side_by_side(xs[g])
            dyg = side_by_side(dys[g])
            dy_ref[at] = dyg
            turned_ref[at] = jnp.dot(permutation(TB), dyg, preferred_element_type=F32).astype(BF16)
            band = shifted_taps(back[g : g + 1], 1)
            bx_ref[at] = with_kinds(band, band[:, LANES:], chunk)
            band = shifted_taps(taps[g : g + 1], 0)
            bdy_ref[at] = with_kinds(band, band[:, :LANES], chunk)


def conv_kernel(chunk, filter_size, info, q_ref, ct_ref, x_ref, turned_ref, taps_ref, bias_ref, rim_ref, mask_ref,
                turned_mask_ref, sel_ref, order_ref, turned_order_ref, *rest):
    out_ref, gq_ref, gf_ref, conv_s, grad_s = rest[-5:]
    width = q_ref.shape[1]
    per = LANES // chunk
    steps = filter_size // TB

    def one(sub, slot, kinds, further):
        depth = (steps + kinds) * TB
        lanes = pl.ds(pl.multiple_of(sub * LANES, LANES), LANES)
        bits, bits32 = chunk_bits(BF16, chunk), chunk_bits(F32, chunk)
        late, lane = TB - 1 - iota((TB, LANES), 0), iota((TB, LANES), 1)
        causal = lane % TB <= late
        rims = to_groups(rim_ref[:, lanes], bits, chunk)
        for g in range(per):
            at = sub * per + g
            xg = x_ref[at]
            ext = rims[g] + [xg[:, i : i + LANES] for i in range(0, xg.shape[1], LANES)]
            window = past_windows(ext, place_of(g, chunk), chunk, steps) + [xg] * (kinds - 1)
            window = jnp.concatenate(window, axis=0) * mask_ref[g, :depth, :]
            y = jnp.dot(band_of(taps_ref[at], kinds)[:, :depth], window, preferred_element_type=F32)
            conv_s[slot, g] = chosen(y, sel_ref, g, kinds) + bias_ref[pl.ds(at, 1), :] * xg.astype(F32)
            turned = jnp.concatenate([turned_ref[at]] * kinds, axis=0) * turned_mask_ref[g, (KINDS - kinds) * TB :, :]
            pairs = lax.dot_general(turned, window, (((1,), (1,)), ((), ())), preferred_element_type=F32)
            pairs = jnp.concatenate([pairs, jnp.zeros((kinds * TB, WIDE - depth), F32)], axis=1)
            far = pairs[(kinds - 1) * TB :, :LANES]
            grad_s[slot, 0, g : g + 1, :] = skew_left(jnp.where(lane > late, far, 0.0))
            own = jnp.zeros((TB, LANES), F32)
            for kind in range(kinds):
                first = (kinds - 1 - kind) * TB
                own = jnp.where(causal & (lane // TB == kind), pairs[first : first + TB, LANES:], own)
            grad_s[slot, 1, g : g + 1, :] = skew_left(own)

        def more(index, carry):
            level, g = index // per, index % per
            at = sub * per + g
            here = order_ref[g] == level.astype(F32)
            xq = jnp.where(here, x_ref[at].astype(F32), 0.0).astype(BF16)
            turned = turned_order_ref[g] == level.astype(F32)
            turned = jnp.where(turned, turned_ref[at].astype(F32), 0.0).astype(BF16)
            own = taps_ref[at][TB : 2 * TB, :TB]
            conv_s[slot, g] += jnp.where(here, jnp.dot(own, xq, preferred_element_type=F32), 0.0)
            pairs = lax.dot_general(turned, xq, (((1,), (1,)), ((), ())), preferred_element_type=F32)
            pairs = jnp.concatenate([pairs, jnp.zeros((TB, LANES - TB), F32)], axis=1)
            grad_s[slot, 1, pl.ds(g, 1), :] += skew_left(jnp.where(causal & (lane < TB), pairs, 0.0))
            return carry

        if further:
            lax.fori_loop(KINDS * per, info[0] * per, more, 0)
        terms, own = grad_s[slot, 0], grad_s[slot, 1]
        last = iota((per, LANES), 1) >= LANES - TB
        for kind in range(kinds):
            shift = (LANES - kind * TB) % LANES
            terms += jnp.where(last, pltpu.roll(own, shift, 1) if shift else own, 0.0)
        gf_ref[pl.ds(pl.multiple_of(sub * per, per), per), :] = terms
        filtered = from_groups([conv_s[slot, g] for g in range(per)], bits32, chunk)
        out_ref[:, lanes] = (q_ref[:, lanes].astype(F32) * filtered).astype(BF16)
        gq_ref[:, lanes] = (ct_ref[:, lanes].astype(F32) * filtered).astype(BF16)

    for_all_lanes(one, width // LANES, info)


def back_kernel(chunk, filter_size, info, k_ref, v_ref, dy_ref, taps_ref, bias_ref, rim_ref, mask_ref, sel_ref,
                order_ref, *rest):
    gk_ref, gv_ref, token_ref, back_s = rest[-4:]
    token_ref[...] = jnp.zeros_like(token_ref)
    width = k_ref.shape[1]
    per = LANES // chunk
    steps = filter_size // TB

    def one(sub, slot, kinds, further):
        depth = (steps + kinds) * TB
        lanes = pl.ds(pl.multiple_of(sub * LANES, LANES), LANES)
        bits, bits32 = chunk_bits(BF16, chunk), chunk_bits(F32, chunk)
        rims = to_groups(rim_ref[:, lanes], bits, chunk)
        for g in range(per):
            at = sub * per + g
            dyg = dy_ref[at]
            ext = [dyg[:, i : i + LANES] for i in range(0, dyg.shape[1], LANES)] + rims[g]
            window = next_windows(ext, place_of(g, chunk), chunk, steps) + [dyg] * (kinds - 1)
            window = jnp.concatenate(window, axis=0) * mask_ref[g, :depth, :]
            y = jnp.dot(band_of(taps_ref[at], kinds)[:, :depth], window, preferred_element_type=F32)
            back_s[slot, g] = chosen(y, sel_ref, g, kinds) + bias_ref[pl.ds(at, 1), :] * dyg.astype(F32)

        def more(index, carry):
            level, g = index // per, index % per
            at = sub * per + g
            here = order_ref[g] == level.astype(F32)
            dyq = jnp.where(here, dy_ref[at].astype(F32), 0.0).astype(BF16)
            own = taps_ref[at][:TB, :TB]
            back_s[slot, g] += jnp.where(here, jnp.dot(own, dyq, preferred_element_type=F32), 0.0)
            return carry

        if further:
            lax.fori_loop(KINDS * per, info[0] * per, more, 0)
        back = from_groups([back_s[slot, g] for g in range(per)], bits32, chunk)
        gk_ref[:, lanes] = (back * v_ref[:, lanes].astype(F32)).astype(BF16)
        gv_ref[:, lanes] = (back * k_ref[:, lanes].astype(F32)).astype(BF16)

    for_all_lanes(one, width // LANES, info)


def for_all_lanes(one, count, info):
    together = math.gcd(count, TOGETHER)

    def run(kinds, further):
        def step(index, carry):
            for slot in range(together):
                one(index * together + slot, slot, kinds, further)
            return carry

        lax.fori_loop(0, count // together, step, 0)

    pl.when(info[0] < KINDS)(lambda: run(KINDS - 1, False))
    pl.when(info[0] == KINDS)(lambda: run(KINDS, False))
    pl.when(info[0] > KINDS)(lambda: run(KINDS, True))


def call(kernel, name, info, count, ins, outs, scratch=(), previous=None, after=()):
    operands = [a for a, _, _ in ins]
    in_specs = [pl.BlockSpec(block, at) for _, block, at in ins]
    aliases = {}
    if previous is not None:
        aliases = {1 + len(operands) + i: i for i in range(len(previous))}
        in_specs += [pl.BlockSpec(memory_space=pl.ANY)] * len(previous)
        operands += list(previous)
    in_specs += [pl.BlockSpec(memory_space=pl.ANY)] * len(after)
    operands += list(after)
    return pl.pallas_call(
        kernel,
        grid_spec=pltpu.PrefetchScalarGridSpec(
            num_scalar_prefetch=1,
            grid=(count,),
            in_specs=in_specs,
            out_specs=[pl.BlockSpec(block, at) for _, _, block, at in outs],
            scratch_shapes=list(scratch),
        ),
        out_shape=[jax.ShapeDtypeStruct(shape, kind) for shape, kind, _, _ in outs],
        input_output_aliases=aliases,
        compiler_params=pltpu.CompilerParams(vmem_limit_bytes=VMEM_BYTES),
        cost_estimate=pl.CostEstimate(flops=2**24, bytes_accessed=2**20, transcendentals=0),
        name=name,
    )(info, *operands)


def wide(array, block, first):
    return (array, (array.shape[0], block), lambda i, c: (0, first + i))


def per_group(array, groups, first):
    rest = array.shape[1:]
    return (array, (groups, *rest), lambda i, c: (first + i, *[0] * len(rest)))


def fixed(array):
    return (array, array.shape, lambda i, c: (0, 0, 0))


def prepare(info, big, filters):
    row_count, channels = big[0].shape
    chunk, block = TB, math.gcd(channels, 512)
    groups, total, filter_size = block // chunk, channels // chunk, filters.shape[1]
    taps = (filters, (groups, filter_size), lambda i, c: (c[0] * (channels // block) + i, 0))
    ins = [wide(a, block, 0) for a in big] + [taps]
    shapes = [(TB, row_count)] * 3 + [((1 + KINDS) * TB, LANES)] * 2
    outs = [((total, *s), BF16, (groups, *s), lambda i, c: (i, 0, 0)) for s in shapes]
    outs.append(((1, channels), F32, (1, block), lambda i, c: (0, i)))
    outs.append(((filter_size, channels), BF16, (filter_size, block), lambda i, c: (0, i)))
    return call(functools.partial(prepare_kernel, chunk), "prepare", info, channels // block, ins, outs)


def run_part(kernel, name, part, parts, info, pair, grouped, rim, rim_first, masks, filter_size, small, previous=None, after=()):
    row_count, channels = pair[0].shape
    chunk, width = TB, channels // parts
    block = math.gcd(width, 512)
    groups, first = block // chunk, part * (width // block)
    per = LANES // chunk
    ins = [wide(a, block, first) for a in pair] + [per_group(a, groups, first) for a in grouped]
    ins += [wide(rim, block, rim_first * (width // block))] + [fixed(a) for a in masks]
    outs = [((row_count, channels), BF16, (row_count, block), lambda i, c: (0, first + i))] * 2
    scratch = [pltpu.VMEM((TOGETHER, per, TB, row_count), F32)]
    if small:
        outs += [((channels // chunk, filter_size), F32, (groups, filter_size), lambda i, c: (first + i, 0))]
        scratch += [pltpu.VMEM((TOGETHER, 2, per, LANES), F32)]
    else:
        outs += [((8, LANES), F32, (8, LANES), lambda i, c: (0, 0))]
    kernel = functools.partial(kernel, chunk, filter_size)
    return call(kernel, name, info, width // block, ins, outs, scratch, previous, after)


def reset_kernel(steps, near_ref, mask_x, turned_x, sel_x, order_x, turned_order_x, mask_dy, sel_dy, order_dy, kinds):
    total = near_ref.shape[1]
    rows = total - steps * TB
    near = jnp.clip(near_ref[...], -1024, 1024).astype(F32)
    lane, row = iota((TB, total), 1), iota((TB, total), 0)
    spread = jnp.where(lane % TB == row, jnp.broadcast_to(near, (TB, total)), 0.0)
    same = flag(iota((total, total), 0) // TB == iota((total, total), 1) // TB, F32)
    begin = jnp.floor(exact_dot(spread, same) + 0.5)
    own = begin[:, :rows]
    block = iota((TB, rows), 1) // TB * TB
    pos = (block + iota((TB, rows), 0)).astype(F32)
    marks = flag((own == pos) & (iota((TB, rows), 0) > 0))
    before = flag(iota((TB, TB), 0) >= iota((TB, TB), 1))
    order = jnp.dot(before, marks, preferred_element_type=F32)
    behind = order[TB - 1 :] - order
    first = jnp.broadcast_to(own[:1], (TB, rows))
    turn = permutation(TB)

    def put(ref, at, value):
        parts = [value[:, i : i + LANES] for i in range(0, rows, LANES)]
        for g in range(ref.shape[0]):
            turned = side_by_side([pltpu.roll(a, g * TB, 1) if g else a for a in parts])
            ref[g, at * TB : (at + 1) * TB, :] = turned.astype(ref.dtype)

    for i in range(steps):
        put(mask_x, i, flag(pos - TB * (steps - i) >= first, F32))
        later = pltpu.roll(begin, total - (i + 1) * TB, 1)[:, :rows]
        put(mask_dy, i + 1, flag(later <= (block + TB - 1).astype(F32), F32))
    for kind in range(KINDS):
        put(mask_x, steps + kind, flag(order == kind, F32))
        put(sel_x, kind, flag(order == kind, F32))
        put(turned_x, KINDS - 1 - kind, jnp.dot(turn, flag(order == kind), preferred_element_type=F32))
        put(mask_dy, steps + kind if kind else 0, flag(behind == kind, F32))
        put(sel_dy, kind, flag(behind == kind, F32))
    put(order_x, 0, order)
    put(order_dy, 0, behind)
    put(turned_order_x, 0, jnp.dot(turn, order.astype(BF16), preferred_element_type=F32))
    kinds[0] = 1 + jnp.max(order).astype(jnp.int32)


def reset_masks(near, row_count, steps):
    depth, high, per = (steps + KINDS) * TB, KINDS * TB, LANES // TB
    shapes = [(depth, BF16), (high, BF16), (high, F32), (TB, F32), (TB, F32), (depth, BF16), (high, F32), (TB, F32)]
    out = pl.pallas_call(
        functools.partial(reset_kernel, steps),
        out_shape=[jax.ShapeDtypeStruct((per, rows, row_count), kind) for rows, kind in shapes]
        + [jax.ShapeDtypeStruct((1,), jnp.int32)],
        out_specs=[pl.BlockSpec(memory_space=pltpu.VMEM)] * len(shapes) + [pl.BlockSpec(memory_space=pltpu.SMEM)],
        compiler_params=pltpu.CompilerParams(vmem_limit_bytes=VMEM_BYTES),
        name="resets",
    )(near)
    return out[:5], out[5:8], out[8]


def passed_along(value, axis, steps):
    count = lax.axis_size(axis)
    initial, last = (max(0, -steps), min(count, count - steps))
    return lax.ppermute(value, axis, [(source, source + steps) for source in range(initial, last)])


def rounds_of_sum(value, axis):
    count = lax.axis_size(axis)
    if count & (count - 1):
        yield [[value], lax.psum(value, axis)]
        return
    step = 1
    while step < count:
        flips = [step] if 2 * step == count else [step, 2 * step, 3 * step]
        state = [[lax.ppermute(value, axis, [(i, i ^ flip) for i in range(count)]) for flip in flips], value]
        yield state
        near, *far = state[0]
        value = value + near
        if far:
            value = value + (far[0] + far[1])
        state[1] = value
        step <<= len(flips).bit_length()
    yield [[value], value]


def rows_of_all(value, axis):
    count = lax.axis_size(axis)
    if count != 2:
        return lax.all_gather(value, axis, axis=0, tiled=True)
    other = lax.ppermute(value, axis, [(0, 1), (1, 0)])
    is_first = lax.axis_index(axis) == 0
    return jnp.concatenate([jnp.where(is_first, value, other), jnp.where(is_first, other, value)], axis=0)


def body(queries, key_branch, value_branch, cotangent, filters, skip_bias, contig_start):
    row_count, channels = queries.shape
    group_total, filter_size = filters.shape
    ctx_count, tp_count = lax.axis_size("ctx"), lax.axis_size("tp")
    shard, tensor = lax.axis_index("ctx"), lax.axis_index("tp")
    token_count = row_count * ctx_count
    chunk = channels * tp_count // group_total
    groups = channels // chunk

    tail = lambda m: m[row_count - filter_size :]
    left = passed_along(product_bf16(tail(key_branch), tail(value_branch)), "ctx", 1)

    starts = jnp.concatenate([contig_start, jnp.full((filter_size,), 2**30, jnp.int32)])
    first = shard * row_count
    near = (lax.dynamic_slice_in_dim(starts, first, row_count + filter_size, 0) - first)[None, :]
    masks_x, masks_dy, kinds = reset_masks(near, row_count, filter_size // TB)
    bias = jnp.tile(skip_bias.reshape(groups, chunk), (1, row_count // TB))
    big = (queries, cotangent, key_branch, value_branch)
    place = tensor.astype(jnp.int32).reshape(1)
    place, kinds, bias = lax.optimization_barrier((place, kinds, bias))
    x, dy, turned, band_x, band_dy, bias_part, head = prepare(place, big, filters)

    left, head = lax.optimization_barrier((left, head))
    right = passed_along(head, "ctx", -1)

    pair, grouped = (queries, cotangent), (x, turned, band_x, bias)
    output, grad_query, filter_part = run_part(
        conv_kernel, "conv", 0, 1, kinds, pair, grouped, left, 0, masks_x, filter_size, True
    )
    terms = jnp.concatenate([filter_part, bias_part.reshape(channels // filter_size, filter_size)], axis=0)

    pair, grouped = (key_branch, value_branch), (dy, band_dy, bias)
    sums = rounds_of_sum(terms, "ctx")
    done, after, state = None, (), None
    for part in range(BACK_PARTS):
        arriving = next(sums, None)
        state = arriving or state
        *done, token = run_part(
            back_kernel, "back", part, BACK_PARTS, kinds, pair, grouped, right, part, masks_dy, filter_size, False, done, after
        )
        if arriving is not None:
            *arriving[0], token = lax.optimization_barrier((*arriving[0], token))
        after = (token,)
    grad_key, grad_value = done
    for state in sums:
        pass
    terms = state[1]
    grad_filter = rows_of_all(terms[:groups], "tp")[:, ::-1] * (1.0 / math.sqrt(token_count * chunk))
    grad_bias = terms[groups:].reshape(channels) * (1.0 / math.sqrt(token_count))
    return (output, grad_query, grad_key, grad_value, grad_filter, grad_bias)


def solution(mesh):
    whole = P("ctx", "tp")
    return jax.shard_map(
        body,
        mesh=mesh,
        in_specs=(whole, whole, whole, whole, P(), P("tp"), P()),
        out_specs=(whole, whole, whole, whole, P(), P("tp")),
        check_vma=False,
    )
```
